256 devices in a mesh: dp: 8 (over z), ctx: 32 (over x, y, core).
Axes of the slice: x: 4, y: 4, z: 8, core: 2. Of those that a mesh axis runs over, the one named last changes fastest.
Arguments:
- query_vectors: bfloat16 [8, 4096, 2048], P('dp', 'ctx'), may hold values from -6 to 6
- key_vectors: bfloat16 [8, 4096, 2048], P('dp', 'ctx'), may hold values from -6 to 6
- value_vectors: bfloat16 [8, 4096, 2048], P('dp', 'ctx'), may hold values from -13 to 13
- output_grad: bfloat16 [8, 4096, 2048], P('dp', 'ctx'), may hold values from -39 to 39
- feature_weight: bfloat16 [2048, 128], replicated, may hold values from -0.5 to 0.5
Outputs:
- attended: bfloat16 [8, 4096, 2048], P('dp', 'ctx')
- query_grad: bfloat16 [8, 4096, 2048], P('dp', 'ctx')
- key_grad: bfloat16 [8, 4096, 2048], P('dp', 'ctx')
- value_grad: bfloat16 [8, 4096, 2048], P('dp', 'ctx')
- weight_grad: float32 [2048, 128], P('ctx')
The draws below stay inside these ranges and needn't reach their ends.
All inputs are finite; a program needn't handle non-finite values.
Results may differ from the reference program's by a relative error of at most 0.0085.
The reference program's roundings to bfloat16 on the way count: a program that leaves them out, or rounds other values in their place, can miss the bound.
Values sent between devices are 32-bit elements; how exact they have to be, the bound alone decides.
A program may use at most 192 MiB of HBM per device.

```python
import math
import jax
import jax.numpy as jnp
from jax import lax

HEADS = 16
HEAD = 128
FEAT = 128
TOK_DEV = 128
SEQS = 8
LENGTH = 4096
N_CTX = 32


def column_scales(key):
    return jnp.exp(jax.random.uniform(key, (HEADS * HEAD,), jnp.float32, 0.0, math.log(10.0))) / 4.64


def draw_value_vectors(key, part):
    key = jax.random.fold_in(key, 7)
    scale_key, noise_key = jax.random.split(key, 2)
    shape = (SEQS, LENGTH, HEADS * HEAD)
    base = jnp.clip(jax.random.normal(noise_key, shape, jnp.float32), -6.0, 6.0)
    return (base * column_scales(scale_key)).astype(jnp.bfloat16)


def draw_output_grad(key, part):
    key = jax.random.fold_in(key, 9)
    scale_key, noise_key = jax.random.split(key, 2)
    shape = (SEQS, LENGTH, HEADS * HEAD)
    base = jnp.clip(jax.random.normal(noise_key, shape, jnp.float32), -6.0, 6.0)
    return (3.0 * base * column_scales(scale_key)).astype(jnp.bfloat16)


def block_scale(key, shape, pieces, low, high):
    gain = 1.0
    for axis_at, shards_of in pieces:
        heights = jax.random.uniform(jax.random.fold_in(jax.random.fold_in(key, 6), axis_at), (shards_of,), jnp.float32, low / len(pieces), high / len(pieces))
        gain = gain * jnp.repeat(jnp.exp(heights), shape[axis_at] // shards_of).reshape((-1,) + (1,) * (len(shape) - 1 - axis_at))
    return gain


def bell_draw(own_key, shape, deviation, most, shards=(), held_as=jnp.bfloat16):
    level = block_scale(own_key, shape, shards, -0.22, 0.18) if shards else 1.0
    result = jax.random.normal(own_key, shape, jnp.float32) * deviation * level
    return jnp.minimum(jnp.maximum(result, -most), most).astype(held_as)


def setup_inputs(seed: int = 0) -> dict:
    key_list = jax.random.split(jax.random.key(seed), 6)
    query_vectors = bell_draw(key_list[0], (SEQS, LENGTH, HEADS * HEAD), 1.0, 6.0, ((0, 8), (1, 32)))
    key_vectors = bell_draw(key_list[1], (SEQS, LENGTH, HEADS * HEAD), 1.0, 6.0, ((0, 8), (1, 32)))
    value_vectors = draw_value_vectors(jax.random.fold_in(key_list[5], 71), 0)
    output_grad = draw_output_grad(jax.random.fold_in(key_list[5], 71), 0)
    feature_weight = bell_draw(key_list[4], (HEADS * HEAD, FEAT), HEAD ** -0.5, 0.5)
    return dict(query_vectors=query_vectors, key_vectors=key_vectors, value_vectors=value_vectors, output_grad=output_grad, feature_weight=feature_weight)


epsilon = 1e-05
highest = lax.Precision.HIGHEST

def feature_map(activation):
    return jax.nn.elu(activation) + 1.0

def feature_slope(activation):
    return jnp.where(activation > 0.0, 1.0, jnp.exp(jnp.minimum(activation, 0.0)))

def rounded(value):
    return lax.optimization_barrier(value.astype(jnp.bfloat16)).astype(jnp.float32)

def contract(pattern, former, latter):
    return jnp.einsum(pattern, former, latter, precision=highest)

def reference(query_vectors, key_vectors, value_vectors, output_grad, feature_weight):
    weights = feature_weight.astype(jnp.float32).reshape(HEADS, HEAD, FEAT)
    block_shape = (N_CTX, TOK_DEV, HEADS, HEAD)
    positions = jnp.arange(TOK_DEV)
    causal = positions[:, None] >= positions[None, :]

    def per_sequence(operands):
        query_seq, key_seq, value_seq, grad_seq = operands
        query_blk = query_seq.astype(jnp.float32).reshape(block_shape)
        key_blk = key_seq.astype(jnp.float32).reshape(block_shape)
        value_blk = value_seq.astype(jnp.float32).reshape(block_shape)
        grad_blk = grad_seq.astype(jnp.float32).reshape(block_shape)
        query_pre = contract('nthe,hef->nthf', query_blk, weights)
        key_pre = contract('nthe,hef->nthf', key_blk, weights)
        query_feat = rounded(feature_map(query_pre))
        key_feat = rounded(feature_map(key_pre))
        local_state = contract('nthf,nthe->nhfe', key_feat, value_blk)
        zero_state = jnp.zeros_like(local_state[:1])
        prefix = jnp.concatenate([zero_state, jnp.cumsum(local_state, axis=0)[:-1]], axis=0)
        scores = contract('nthf,nuhf->nhtu', query_feat, key_feat)
        score_low = rounded(jnp.where(causal, scores, 0.0))
        numerator = contract('nthf,nhfe->nthe', query_feat, prefix) + contract('nhtu,nuhe->nthe', score_low, value_blk)
        scale_inv = lax.rsqrt(lax.optimization_barrier(jnp.mean(numerator * numerator, axis=-1, keepdims=True)) + epsilon)
        normed = numerator * scale_inv
        grad_numer = rounded(scale_inv * (grad_blk - normed * lax.optimization_barrier(jnp.mean(grad_blk * normed, axis=-1, keepdims=True))))
        back_scores = rounded(jnp.where(causal, contract('nthe,nuhe->nhtu', grad_numer, value_blk), 0.0))
        local_grad = contract('nthf,nthe->nhfe', query_feat, grad_numer)
        reversed_sum = jnp.cumsum(local_grad[::-1], axis=0)[::-1]
        suffix = jnp.concatenate([reversed_sum[1:], jnp.zeros_like(local_grad[:1])], axis=0)
        query_feat_grad = contract('nhfe,nthe->nthf', prefix, grad_numer) + contract('nhtu,nuhf->nthf', back_scores, key_feat)
        key_feat_grad = contract('nhfe,nthe->nthf', suffix, value_blk) + contract('nhtu,nthf->nuhf', back_scores, query_feat)
        value_grad = contract('nhfe,nthf->nthe', suffix, key_feat) + contract('nhtu,nthe->nuhe', score_low, grad_numer)
        query_pre_grad = rounded(query_feat_grad * feature_slope(query_pre))
        key_pre_grad = rounded(key_feat_grad * feature_slope(key_pre))
        query_grad = contract('nthf,hef->nthe', query_pre_grad, weights)
        key_grad = contract('nthf,hef->nthe', key_pre_grad, weights)
        weight_part = contract('nthe,nthf->hef', query_blk, query_pre_grad) + contract('nthe,nthf->hef', key_blk, key_pre_grad)
        flat_shape = (LENGTH, HEADS * HEAD)
        return (normed.astype(jnp.bfloat16).reshape(flat_shape), query_grad.astype(jnp.bfloat16).reshape(flat_shape), key_grad.astype(jnp.bfloat16).reshape(flat_shape), value_grad.astype(jnp.bfloat16).reshape(flat_shape), weight_part)
    results = lax.map(per_sequence, (query_vectors, key_vectors, value_vectors, output_grad))
    weight_grad = lax.optimization_barrier(jnp.sum(results[4], axis=0)).reshape(HEADS * HEAD, FEAT)
    return (results[0], results[1], results[2], results[3], weight_grad)
```

```python
import functools

import jax
import jax.numpy as jnp
from jax import lax
from jax.experimental import pallas as pl
from jax.experimental.pallas import tpu as pltpu
from jax.sharding import PartitionSpec as P

HEAD = 128
EPS = 1e-05
MESH = pl.DeviceIdType.MESH
BF = jnp.bfloat16
F32 = jnp.float32


def dot(a, b, ca, cb):
    return lax.dot_general(a, b, (((ca,), (cb,)), ((), ())), preferred_element_type=F32)


def split(x):
    high = x.astype(BF)
    return high, (x - high.astype(F32)).astype(BF)


def kernel(
    n_dp, n_chip, heads, groups, tok,
    q_hbm, k_hbm, v_hbm, g_hbm, w_hbm,
    att_hbm, dq_hbm, dk_hbm, dv_hbm, wg_hbm,
    q_ref, k_ref, v_ref, g_ref, w_ref,
    att_ref, dq_ref, dk_ref, dv_ref, wg_ref,
    qf_ref, kf_ref, sq_ref, sk_ref, sc_ref, nl_ref, m_ref, dkl_ref, dvl_ref,
    state, sib, pair, gat, pre, ret, oth, sib2,
    wl_ref, wsib, wpair, wgat, zsrc, zgat, zsum,
    in_sem, w_sem, out_sem,
    s_sib, r_sib, s_gat, r_gat, s_ret, r_ret, s_sib2, r_sib2,
    s_ws, r_ws, s_wg, r_wg, s_z1, r_z1, s_z2, r_z2,
):
    dp = lax.axis_index("dp")
    ctx = lax.axis_index("ctx")
    chip, core = lax.div(ctx, 2), lax.rem(ctx, 2)
    sibling = ctx + 1 - 2 * core
    per = heads // groups
    half = per // 2
    rows = half * HEAD
    piece = rows // n_chip
    hw = HEAD // 2

    def peer(d):
        other = lax.rem(chip + d, n_chip)
        return other, other * 2 + core

    def remote(src, dst, ssem, rsem, device):
        return pltpu.make_async_remote_copy(
            src_ref=src, dst_ref=dst, send_sem=ssem, recv_sem=rsem,
            device_id=device, device_id_type=MESH,
        )

    def cols(h, n=1):
        return pl.ds(pl.multiple_of(h * HEAD, HEAD), n * HEAD)

    loads = []
    w_load = pltpu.make_async_copy(w_hbm, w_ref, w_sem)
    w_load.start()
    for g in range(groups):
        cs = pl.ds(g * per * HEAD, per * HEAD)
        mine = []
        for i, (src, dst) in enumerate(
            ((k_hbm, k_ref), (q_hbm, q_ref), (v_hbm, v_ref), (g_hbm, g_ref))
        ):
            c = pltpu.make_async_copy(src.at[0, :, cs], dst.at[:, cs], in_sem.at[g, i])
            c.start()
            mine.append(c)
        loads.append(mine)

    barrier = pltpu.get_barrier_semaphore()

    def greet(device):
        pl.semaphore_signal(barrier, inc=1, device_id=device, device_id_type=MESH)

    greet((dp, sibling))

    @pl.loop(1, n_chip)
    def _(d):
        greet((dp, peer(d)[1]))

    @pl.loop(1, n_dp)
    def _(d):
        greet((lax.rem(dp + d, n_dp), ctx))

    rowid = lax.broadcasted_iota(jnp.int32, (tok, tok), 0)
    colid = lax.broadcasted_iota(jnp.int32, (tok, tok), 1)
    causal = rowid >= colid

    def phi(z):
        return jnp.where(z > 0.0, z + 1.0, jnp.exp(jnp.minimum(z, 0.0)))

    def each(g, body):
        @pl.loop(g * per // 2, (g + 1) * per // 2)
        def _(i):
            body(2 * i)
            body(2 * i + 1)

    def forward_state(h):
        c = cols(h)
        z = dot(k_ref[:, c], w_ref[c, :], 1, 0)
        f = phi(z)
        kf = f.astype(BF)
        kf_ref[:, c] = kf
        sk_ref[:, c] = jnp.minimum(f, 1.0)
        state[0, c, :] = dot(kf, v_ref[:, c], 0, 0)

    def forward_local(h):
        c = cols(h)
        z = dot(q_ref[:, c], w_ref[c, :], 1, 0)
        f = phi(z)
        qf = f.astype(BF)
        qf_ref[:, c] = qf
        sq_ref[:, c] = jnp.minimum(f, 1.0)
        w = jnp.where(causal, dot(qf, kf_ref[:, c], 1, 1), 0.0).astype(BF)
        sc_ref[:, c] = w
        nl_ref[:, c] = dot(w, v_ref[:, c], 1, 0)

    def numer(h):
        c = cols(h)
        qf = qf_ref[:, c]
        ph, plo = split(state[0, c, :])
        n = dot(qf, ph, 1, 0) + dot(qf, plo, 1, 0) + nl_ref[:, c]
        r = lax.rsqrt(jnp.mean(n * n, axis=-1, keepdims=True) + EPS)
        normed = n * r
        att_ref[:, c] = normed.astype(BF)
        og = g_ref[:, c].astype(F32)
        m = (r * (og - normed * jnp.mean(og * normed, axis=-1, keepdims=True))).astype(BF)
        m_ref[:, c] = m
        state[1, c, :] = dot(qf, m, 0, 0)

    def back_local(h):
        c = cols(h)
        m, qf, kf = m_ref[:, c], qf_ref[:, c], kf_ref[:, c]
        ph, plo = split(state[0, c, :])
        b = jnp.where(causal, dot(m, v_ref[:, c], 1, 1), 0.0).astype(BF)
        qg = dot(m, ph, 1, 1) + dot(m, plo, 1, 1) + dot(b, kf, 1, 0)
        qp = (qg * sq_ref[:, c]).astype(BF)
        dq_ref[:, c] = dot(qp, w_ref[c, :], 1, 1).astype(BF)
        wl_ref[c, :] = dot(q_ref[:, c], qp, 0, 0)
        dkl_ref[:, c] = dot(b, qf, 0, 0)
        dvl_ref[:, c] = dot(sc_ref[:, c], m, 0, 0)

    def back_final(h):
        c = cols(h)
        qh, ql = split(state[1, c, :])
        v, kf = v_ref[:, c], kf_ref[:, c]
        kg = dot(v, qh, 1, 1) + dot(v, ql, 1, 1) + dkl_ref[:, c]
        kp = (kg * sk_ref[:, c]).astype(BF)
        dk_ref[:, c] = dot(kp, w_ref[c, :], 1, 1).astype(BF)
        dv_ref[:, c] = (dot(kf, qh, 1, 0) + dot(kf, ql, 1, 0) + dvl_ref[:, c]).astype(BF)
        wl_ref[c, :] += dot(k_ref[:, c], kp, 0, 0)

    def mine_rows(g):
        return pl.ds(pl.multiple_of((g * per + core * half) * HEAD, HEAD), rows)

    def other_rows(g):
        return pl.ds(pl.multiple_of((g * per + (1 - core) * half) * HEAD, HEAD), rows)

    def scan_sib(e, g):
        remote(
            state.at[e, other_rows(g), :], sib.at[e, g], s_sib.at[e, g], r_sib.at[e, g],
            (dp, sibling),
        ).start()

    def own_piece():
        return pl.ds(pl.multiple_of(chip * piece, piece), piece)

    def scan_gather(e, g):
        remote(
            sib.at[e, g], sib.at[e, g], s_sib.at[e, g], r_sib.at[e, g], (dp, sibling)
        ).wait_recv()
        pair[e, g] = state[e, mine_rows(g), :] + sib[e, g]

        @pl.loop(1, n_chip)
        def _(d):
            other, device = peer(d)
            remote(
                pair.at[e, g, pl.ds(pl.multiple_of(other * piece, piece), piece), :],
                gat.at[e, g, chip], s_gat.at[e, g], r_gat.at[e, g], (dp, device),
            ).start()

        gat[e, g, chip] = pair[e, g, own_piece(), :]

    def bulk(buf, ssem, rsem):
        return remote(buf, buf, ssem, rsem, (dp, sibling))

    def scan_return(e, g):
        bulk(gat.at[e, g, pl.ds(0, n_chip - 1)], s_gat.at[e, g], r_gat.at[e, g]).wait_recv()
        order = range(n_chip) if e == 0 else range(n_chip - 1, -1, -1)
        total = jnp.zeros((piece, HEAD), F32)
        for p in order:
            pre[e, g, p] = total
            total = total + gat[e, g, p]

        @pl.loop(1, n_chip)
        def _(d):
            other, device = peer(d)
            remote(
                pre.at[e, g, other], ret.at[e, g, own_piece(), :],
                s_ret.at[e, g], r_ret.at[e, g], (dp, device),
            ).start()

        ret[e, g, own_piece(), :] = pre[e, g, chip]

    def scan_share(e, g):
        span = (n_chip - 1) * piece
        bulk(ret.at[e, g, pl.ds(0, span), :], s_ret.at[e, g], r_ret.at[e, g]).wait_recv()
        base = ret[e, g]
        local = state[e, mine_rows(g), :]
        near = sib[e, g]
        give = (core == 0) if e == 0 else (core == 1)
        oth[e, g] = base + jnp.where(give, local, 0.0)
        remote(
            oth.at[e, g], sib2.at[e, g], s_sib2.at[e, g], r_sib2.at[e, g], (dp, sibling)
        ).start()
        state[e, mine_rows(g), :] = base + jnp.where(give, 0.0, near)

    def scan_done(e, g):
        bulk(sib.at[e, g], s_sib.at[e, g], r_sib.at[e, g]).wait_send()
        bulk(sib2.at[e, g], s_sib2.at[e, g], r_sib2.at[e, g]).wait_recv()
        state[e, other_rows(g), :] = sib2[e, g]

    def head_half(h, c):
        return pl.ds(pl.multiple_of(h * HEAD + c * hw, hw), hw)

    def weight_sib(g):
        for i in range(per):
            wpair[1, g, i] = wl_ref[head_half(g * per + i, 1 - core), :]
        remote(wpair.at[1, g], wsib.at[g], s_ws.at[g], r_ws.at[g], (dp, sibling)).start()

    def weight_gather(g):
        bulk(wsib.at[g], s_ws.at[g], r_ws.at[g]).wait_recv()
        for i in range(per):
            h = g * per + i
            wpair[0, g, i] = wl_ref[head_half(h, core), :] + wsib[g, i]

            @pl.when(chip != h)
            def _():
                remote(
                    wpair.at[0, g, i], wgat.at[chip], s_wg.at[g], r_wg, (dp, 2 * h + core)
                ).start()

            @pl.when(chip == h)
            def _():
                wgat[chip] = wpair[0, g, i]

    def weight_finish():
        bulk(wgat.at[pl.ds(0, n_chip - 1)], s_wg.at[0], r_wg).wait_recv()
        total = wgat[0]
        for p in range(1, n_chip):
            total = total + wgat[p]
        zsrc[...] = total.reshape(n_dp, hw // n_dp, HEAD)

        @pl.loop(1, n_dp)
        def _(d):
            other = lax.rem(dp + d, n_dp)
            remote(zsrc.at[other], zgat.at[dp], s_z1, r_z1, (other, ctx)).start()

        zgat[dp] = zsrc[dp]
        bulk(zgat.at[pl.ds(0, n_dp - 1)], s_z1, r_z1).wait_recv()
        total = zgat[0]
        for z in range(1, n_dp):
            total = total + zgat[z]
        zsum[...] = total

        @pl.loop(1, n_dp)
        def _(d):
            other = lax.rem(dp + d, n_dp)
            remote(zsum, wg_ref.at[dp], s_z2, r_z2, (other, ctx)).start()

        wg_ref[dp] = total
        bulk(wg_ref.at[pl.ds(0, n_dp - 1)], s_z2, r_z2).wait_recv()

    stores = []

    def store(i, g, src, dst):
        cs = pl.ds(g * per * HEAD, per * HEAD)
        c = pltpu.make_async_copy(src.at[:, cs], dst.at[0, :, cs], out_sem.at[i, g])
        c.start()
        stores.append(c)

    G = range(groups)
    w_load.wait()
    for g in G:
        loads[g][0].wait()
        loads[g][2].wait()
        each(g, forward_state)
        if g == 0:
            pl.semaphore_wait(barrier, 1 + (n_chip - 1) + (n_dp - 1))
        scan_sib(0, g)
    for g in G:
        scan_gather(0, g)
    for g in G:
        loads[g][1].wait()
        each(g, forward_local)
    for g in G:
        scan_return(0, g)
    for g in G:
        scan_share(0, g)
    for g in G:
        scan_done(0, g)
        loads[g][3].wait()
        each(g, numer)
        store(0, g, att_ref, att_hbm)
        scan_sib(1, g)
    for g in G:
        scan_gather(1, g)
    each(0, back_local)
    for g in G:
        scan_return(1, g)
    for g in range(1, groups):
        each(g, back_local)
    for g in G:
        store(1, g, dq_ref, dq_hbm)
    for g in G:
        scan_share(1, g)
    for g in G:
        scan_done(1, g)
        each(g, back_final)
        weight_sib(g)
        store(2, g, dk_ref, dk_hbm)
        store(3, g, dv_ref, dv_hbm)
    for g in G:
        weight_gather(g)
    weight_finish()
    wg_out = pltpu.make_async_copy(wg_ref, wg_hbm, w_sem)
    wg_out.start()

    for g in G:
        for e in range(2):
            bulk(gat.at[e, g, pl.ds(0, n_chip - 1)], s_gat.at[e, g], r_gat.at[e, g]).wait_send()
            bulk(pre.at[e, g, pl.ds(0, n_chip - 1)], s_ret.at[e, g], r_ret.at[e, g]).wait_send()
            bulk(oth.at[e, g], s_sib2.at[e, g], r_sib2.at[e, g]).wait_send()
        bulk(wsib.at[g], s_ws.at[g], r_ws.at[g]).wait_send()
        inside = (chip >= g * per) & (chip < (g + 1) * per)

        @pl.when(inside)
        def _():
            bulk(wpair.at[0, g, pl.ds(0, per - 1)], s_wg.at[g], r_wg).wait_send()

        @pl.when(jnp.logical_not(inside))
        def _():
            bulk(wpair.at[0, g], s_wg.at[g], r_wg).wait_send()

    bulk(zsrc.at[pl.ds(0, n_dp - 1)], s_z1, r_z1).wait_send()
    bulk(wg_ref.at[pl.ds(0, n_dp - 1)], s_z2, r_z2).wait_send()
    for c in stores:
        c.wait()
    wg_out.wait()


def body(n_dp, n_ctx, groups, q, k, v, g, w):
    _, tok, width = q.shape
    heads = width // HEAD
    n_chip = n_ctx // 2
    per = heads // groups
    rows = per // 2 * HEAD
    piece = rows // n_chip
    hw = HEAD // 2
    act = pltpu.VMEM((tok, width), BF)
    wide = pltpu.VMEM((tok, width), F32)
    dma = pltpu.SemaphoreType.DMA
    block = pltpu.VMEM((2, groups, rows, HEAD), F32)
    slots = pltpu.VMEM((2, groups, n_chip, piece, HEAD), F32)
    scratch = (
        [act] * 4 + [pltpu.VMEM((width, HEAD), BF)]
        + [act] * 4 + [pltpu.VMEM((n_dp, hw // n_dp, HEAD), F32)]
        + [act, act, wide, wide, act, wide, act, wide, wide]
        + [pltpu.VMEM((2, width, HEAD), F32), block, block, slots, slots, block, block, block]
        + [
            pltpu.VMEM((width, HEAD), F32),
            pltpu.VMEM((groups, per, hw, HEAD), F32),
            pltpu.VMEM((2, groups, per, hw, HEAD), F32),
            pltpu.VMEM((n_chip, hw, HEAD), F32),
            pltpu.VMEM((n_dp, hw // n_dp, HEAD), F32),
            pltpu.VMEM((n_dp, hw // n_dp, HEAD), F32),
            pltpu.VMEM((hw // n_dp, HEAD), F32),
        ]
        + [dma((groups, 4)), dma, dma((4, groups))]
        + [dma((2, groups))] * 8
        + [dma((groups,))] * 3 + [dma] * 5
    )
    out = jax.ShapeDtypeStruct(q.shape, BF)
    hbm = pl.BlockSpec(memory_space=pl.ANY)
    att, dq, dk, dv, wg = pl.pallas_call(
        functools.partial(kernel, n_dp, n_chip, heads, groups, tok),
        out_shape=[out] * 4 + [jax.ShapeDtypeStruct((n_dp, hw // n_dp, HEAD), F32)],
        in_specs=[hbm] * 5,
        out_specs=[hbm] * 5,
        scratch_shapes=scratch,
        compiler_params=pltpu.CompilerParams(
            collective_id=0, has_side_effects=True, vmem_limit_bytes=48 * 1024 * 1024
        ),
        cost_estimate=pl.CostEstimate(
            flops=40 * heads * HEAD**3, bytes_accessed=5 * 2**20, transcendentals=0
        ),
    )(q, k, v, g, w)
    return att, dq, dk, dv, wg.reshape(hw, HEAD)


def solution(mesh):
    n_dp, n_ctx = mesh.shape["dp"], mesh.shape["ctx"]
    spec = P("dp", "ctx", None)
    return jax.shard_map(
        functools.partial(body, n_dp, n_ctx, 2),
        mesh=mesh,
        in_specs=(spec, spec, spec, spec, P()),
        out_specs=(spec, spec, spec, spec, P("ctx", None)),
        check_vma=False,
    )
```

```python
import functools

import jax
import jax.numpy as jnp
from jax import lax
from jax.experimental import pallas as pl
from jax.experimental.pallas import tpu as pltpu
from jax.sharding import PartitionSpec as P

HEAD = 128
ORDER = (
    "fs0", "fs1", "fs2", "fs3", "b00", "b01", "b02", "b03", "fl0", "fl1", "fl2", "fl3", "c00",
    "c01", "c02", "c03", "e00", "e01", "nu0", "e02", "nu1", "b10", "e03", "nu2", "b11", "nu3",
    "b12", "bl0", "b13", "bl1", "bl2", "c10", "bl3", "c11", "c12", "c13", "e10", "e11", "bf0",
    "e12", "bf1", "wb0", "e13", "bf2", "wb1", "bf3", "wb2", "wb3",
)
EPS = 1e-05
SIDE = 4
PER = 4
FAR_FIRST = sorted(
    [(x, y) for x in range(SIDE) for y in range(SIDE) if x or y],
    key=lambda d: -sum(min(s, SIDE - s) for s in d),
)
MESH = pl.DeviceIdType.MESH
BF = jnp.bfloat16
F32 = jnp.float32


def dot(a, b, ca, cb):
    return lax.dot_general(a, b, (((ca,), (cb,)), ((), ())), preferred_element_type=F32)


def split(x):
    high = x.astype(BF)
    return high, (x - high.astype(F32)).astype(BF)


def phi(z):
    return jnp.where(z > 0.0, z + 1.0, jnp.exp(jnp.minimum(z, 0.0)))


def write_out(*refs):
    src, dst, mid, sems = refs[:5], refs[5:10], refs[10:15], refs[15]
    ins = [pltpu.make_async_copy(src[i], mid[i], sems.at[0, i]) for i in range(5)]
    outs = [pltpu.make_async_copy(mid[i], dst[i], sems.at[1, i]) for i in range(5)]
    for c in ins:
        c.start()
    for a, b in zip(ins, outs):
        a.wait()
        b.start()
    for c in outs:
        c.wait()


def kernel(
    n_dp, heads, tok,
    q_hbm, k_hbm, v_hbm, g_hbm, w_hbm,
    att_hbm, dq_hbm, dk_hbm, dv_hbm, wg_hbm,
    q_ref, k_ref, v_ref, g_ref, w_ref,
    att_ref, dq_ref, dk_ref, dv_ref, wg_ref,
    qf_ref, kf_ref, sq_ref, sk_ref, sct_ref, nl_ref, m_ref, dkl_ref, dvl_ref,
    state, full, sib, pair, ygat, pre, ret, oth,
    wl_ref, wsib, wpair, wgat, zsrc, zgat,
    in_sem, w_sem, out_sem,
    s_sib, r_sib, s_y, r_y, s_ret, r_ret, s_sib2, r_sib2,
    s_ws, r_ws, s_wg, r_wg, s_z, r_z, near_sem, far_sem,
):
    dp = lax.axis_index("dp")
    ctx = lax.axis_index("ctx")
    core = lax.rem(ctx, 2)
    chip = lax.div(ctx, 2)
    cx, cy = lax.div(chip, SIDE), lax.rem(chip, SIDE)
    sibling = ctx + 1 - 2 * core
    groups = heads // PER
    rows = PER // 2 * HEAD
    piece = rows // (SIDE * SIDE)
    hw = HEAD // 2
    n_chip = SIDE * SIDE

    def plane(dx, dy):
        o = lax.rem(cx + dx, SIDE) * SIDE + lax.rem(cy + dy, SIDE)
        return o, (dp, o * 2 + core)

    def zline(d):
        return (lax.rem(dp + d, n_dp), ctx)

    near = (dp, sibling)

    def remote(src, dst, ssem, rsem, where):
        return pltpu.make_async_remote_copy(
            src_ref=src, dst_ref=dst, send_sem=ssem, recv_sem=rsem,
            device_id=where, device_id_type=MESH,
        )

    def bulk(buf, ssem, rsem):
        return remote(buf, buf, ssem, rsem, near)

    def members(g):
        turn, first = divmod(g * PER, SIDE)
        return [SIDE * i + (i + turn) % SIDE for i in range(first, first + PER)]

    def cols(h):
        return pl.ds(h * HEAD, HEAD)

    def place(g, i):
        return pl.ds((g * PER + i) * HEAD, HEAD)

    w_load = pltpu.make_async_copy(w_hbm, w_ref, w_sem)
    w_load.start()
    loads = []
    for i, (src, dst) in enumerate(
        ((k_hbm, k_ref), (v_hbm, v_ref), (q_hbm, q_ref), (g_hbm, g_ref))
    ):
        loads.append(pltpu.make_async_copy(src.at[0], dst, in_sem.at[i]))
    loads[0].start()
    loads[1].start()

    barrier = pltpu.get_barrier_semaphore()

    def greet(sem, where):
        pl.semaphore_signal(sem, inc=1, device_id=where, device_id_type=MESH)

    greet(barrier, near)
    for d in FAR_FIRST:
        greet(barrier, plane(*d)[1])
    greet(barrier, zline(1))
    greet(barrier, zline(n_dp - 1))

    def enter():
        loads[2].start()
        loads[3].start()
        pl.semaphore_wait(barrier, 1 + len(FAR_FIRST) + 2)
        greet(near_sem, zline(1))
        greet(near_sem, zline(n_dp - 1))

    def relay():
        pl.semaphore_wait(near_sem, 2)
        greet(far_sem, zline(2))
        greet(far_sem, zline(n_dp - 2))

    def relayed():
        pl.semaphore_wait(far_sem, 2)

    rowid = lax.broadcasted_iota(jnp.int32, (tok, tok), 0)
    colid = lax.broadcasted_iota(jnp.int32, (tok, tok), 1)
    causal = rowid >= colid
    causal_t = rowid <= colid

    def lockstep(g, body):
        running = [body(g, i, h) for i, h in enumerate(members(g))]
        while running:
            alive = []
            for r in running:
                try:
                    next(r)
                    alive.append(r)
                except StopIteration:
                    pass
            running = alive

    def forward_state(g, i, h):
        c = cols(h)
        z = dot(k_ref[:, c], w_ref[c, :], 1, 0)
        yield
        f = phi(z)
        kf = f.astype(BF)
        kf_ref[:, c] = kf
        sk_ref[:, c] = jnp.minimum(f, 1.0)
        yield
        state[0, place(g, i), :] = dot(kf, v_ref[:, c], 0, 0)

    def forward_local(g, i, h):
        c = cols(h)
        z = dot(q_ref[:, c], w_ref[c, :], 1, 0)
        yield
        f = phi(z)
        qf = f.astype(BF)
        qf_ref[:, c] = qf
        sq_ref[:, c] = jnp.minimum(f, 1.0)
        yield
        kf = kf_ref[:, c]
        w = jnp.where(causal, dot(qf, kf, 1, 1), 0.0).astype(BF)
        sct_ref[:, c] = jnp.where(causal_t, dot(kf, qf, 1, 1), 0.0).astype(BF)
        yield
        nl_ref[:, c] = dot(w, v_ref[:, c], 1, 0)

    def numer(g, i, h):
        c = cols(h)
        qf = qf_ref[:, c]
        ph, plo = split(full[0, place(g, i), :])
        yield
        n = dot(qf, ph, 1, 0) + dot(qf, plo, 1, 0) + nl_ref[:, c]
        yield
        r = lax.rsqrt(jnp.mean(n * n, axis=-1, keepdims=True) + EPS)
        yield
        normed = n * r
        att_ref[:, c] = normed.astype(BF)
        og = g_ref[:, c].astype(F32)
        s = jnp.mean(og * normed, axis=-1, keepdims=True)
        yield
        m = (r * (og - normed * s)).astype(BF)
        m_ref[:, c] = m
        yield
        state[1, place(g, i), :] = dot(qf, m, 0, 0)

    def back_local(g, i, h):
        c = cols(h)
        m, qf, kf, v = m_ref[:, c], qf_ref[:, c], kf_ref[:, c], v_ref[:, c]
        ph, plo = split(full[0, place(g, i), :])
        b = jnp.where(causal, dot(m, v, 1, 1), 0.0).astype(BF)
        bt = jnp.where(causal_t, dot(v, m, 1, 1), 0.0).astype(BF)
        yield
        qg = dot(m, ph, 1, 1) + dot(m, plo, 1, 1) + dot(b, kf, 1, 0)
        dkl_ref[:, c] = dot(bt, qf, 1, 0)
        dvl_ref[:, c] = dot(sct_ref[:, c], m, 1, 0)
        yield
        qp = (qg * sq_ref[:, c]).astype(BF)
        yield
        dq_ref[:, c] = dot(qp, w_ref[c, :], 1, 1).astype(BF)
        wl_ref[place(g, i), :] = dot(q_ref[:, c], qp, 0, 0)

    def back_final(g, i, h):
        c = cols(h)
        qh, ql = split(full[1, place(g, i), :])
        v, kf = v_ref[:, c], kf_ref[:, c]
        yield
        kg = dot(v, qh, 1, 1) + dot(v, ql, 1, 1) + dkl_ref[:, c]
        dv_ref[:, c] = (dot(kf, qh, 1, 0) + dot(kf, ql, 1, 0) + dvl_ref[:, c]).astype(BF)
        yield
        kp = (kg * sk_ref[:, c]).astype(BF)
        yield
        dk_ref[:, c] = dot(kp, w_ref[c, :], 1, 1).astype(BF)
        wl_ref[place(g, i), :] += dot(k_ref[:, c], kp, 0, 0)

    def half_rows(g, c):
        return pl.ds(pl.multiple_of(g * PER * HEAD + c * rows, rows), rows)

    def part(o):
        return pl.ds(pl.multiple_of(o * piece, piece), piece)

    def scan_a(e, g):
        remote(
            state.at[e, half_rows(g, 1 - core), :], sib.at[e, g],
            s_sib.at[e, g], r_sib.at[e, g], near,
        ).start()

    def scan_b(e, g):
        bulk(sib.at[e, g], s_sib.at[e, g], r_sib.at[e, g]).wait_recv()
        pair[e, g] = state[e, half_rows(g, core), :] + sib[e, g]
        for d in FAR_FIRST:
            o, where = plane(*d)
            remote(
                pair.at[e, g, part(o), :], ygat.at[e, g, chip],
                s_y.at[e, g], r_y.at[e, g], where,
            ).start()
        ygat[e, g, chip] = pair[e, g, part(chip), :]

    def scan_c(e, g):
        bulk(ygat.at[e, g, pl.ds(0, n_chip - 1)], s_y.at[e, g], r_y.at[e, g]).wait_recv()
        order = range(n_chip) if e == 0 else range(n_chip - 1, -1, -1)
        total = jnp.zeros((piece, HEAD), F32)
        for p in order:
            pre[e, g, p] = total
            total = total + ygat[e, g, p]
        for d in FAR_FIRST:
            o, where = plane(*d)
            remote(
                pre.at[e, g, o], ret.at[e, g, part(chip), :],
                s_ret.at[e, g], r_ret.at[e, g], where,
            ).start()
        ret[e, g, part(chip), :] = pre[e, g, chip]

    def scan_e(e, g):
        bulk(
            ret.at[e, g, pl.ds(0, rows - piece), :], s_ret.at[e, g], r_ret.at[e, g]
        ).wait_recv()
        base = ret[e, g]
        local = state[e, half_rows(g, core), :]
        give = core == e
        oth[e, g] = base + jnp.where(give, local, 0.0)
        remote(
            oth.at[e, g], full.at[e, half_rows(g, core), :],
            s_sib2.at[e, g], r_sib2.at[e, g], near,
        ).start()
        full[e, half_rows(g, core), :] = base + jnp.where(give, 0.0, sib[e, g])

    def scan_f(e, g):
        bulk(sib.at[e, g], s_sib2.at[e, g], r_sib2.at[e, g]).wait_recv()

    def weight_a(g):
        for i in range(PER):
            wpair[1, g, i] = wl_ref[
                pl.ds(pl.multiple_of((g * PER + i) * HEAD + (1 - core) * hw, hw), hw), :
            ]
        remote(wpair.at[1, g], wsib.at[g], s_ws.at[g], r_ws.at[g], near).start()

    def weight_b(g):
        bulk(wsib.at[g], s_ws.at[g], r_ws.at[g]).wait_recv()
        for i, h in enumerate(members(g)):
            wpair[0, g, i] = (
                wl_ref[pl.ds(pl.multiple_of((g * PER + i) * HEAD + core * hw, hw), hw), :]
                + wsib[g, i]
            )
        for i, h in enumerate(members(g)):

            @pl.when(chip != h)
            def _():
                remote(
                    wpair.at[0, g, i], wgat.at[chip], s_wg.at[g, i], r_wg, (dp, 2 * h + core)
                ).start()

            @pl.when(chip == h)
            def _():
                wgat[chip] = wpair[0, g, i]

    def weight_c():
        bulk(wgat.at[pl.ds(0, n_chip - 1)], s_z, r_wg).wait_recv()
        total = wgat[0]
        for p in range(1, n_chip):
            total = total + wgat[p]
        zsrc[...] = total
        for d in (4, 3, 5, 2, 6, 1, 7):
            remote(zsrc, zgat.at[dp], s_z, r_z, zline(d)).start()
        zgat[dp] = total
        bulk(zgat.at[pl.ds(0, n_dp - 1)], s_z, r_z).wait_recv()
        total = zgat[0]
        for z in range(1, n_dp):
            total = total + zgat[z]
        wg_ref[...] = total

    stores = []

    def store(i, src, dst):
        c = pltpu.make_async_copy(src, dst.at[0], out_sem.at[i])
        c.start()
        stores.append(c)

    def fs(g):
        lockstep(g, forward_state)
        if g == 0:
            enter()
        scan_a(0, g)

    def fl(g):
        lockstep(g, forward_local)

    def nu(g):
        scan_f(0, g)
        lockstep(g, numer)
        scan_a(1, g)

    def bl(g):
        lockstep(g, back_local)

    def bf(g):
        scan_f(1, g)
        lockstep(g, back_final)
        weight_a(g)

    first = [False] * 4

    def once(i, action):
        if not first[i]:
            first[i] = True
            action()

    def step(word):
        name, g = word[:-1], int(word[-1])
        if name == "fl":
            once(0, lambda: (loads[2].wait(), relay()))
            fl(g)
        elif name == "nu":
            once(1, lambda: (loads[3].wait(), relayed()))
            nu(g)
        elif name in ("fs", "bl", "bf", "wb"):
            {"fs": fs, "bl": bl, "bf": bf, "wb": weight_b}[name](g)
        else:
            {"b": scan_b, "c": scan_c, "e": scan_e}[name[0]](int(name[1]), g)

    w_load.wait()
    loads[0].wait()
    loads[1].wait()
    left = list(ORDER)
    while left:
        step(left.pop(0))
        names = [w[:-1] for w in left]
        if "nu" not in names:
            once(2, lambda: store(0, att_ref, att_hbm))
        if "bl" not in names:
            once(3, lambda: store(1, dq_ref, dq_hbm))
        if names and names[0] == "wb" and "bf" not in names and len(stores) == 2:
            store(2, dk_ref, dk_hbm)
            store(3, dv_ref, dv_hbm)
    weight_c()
    wg_out = pltpu.make_async_copy(wg_ref, wg_hbm, w_sem)
    wg_out.start()

    for g in range(groups):
        for e in range(2):
            bulk(ygat.at[e, g, pl.ds(0, n_chip - 1)], s_y.at[e, g], r_y.at[e, g]).wait_send()
            bulk(pre.at[e, g, pl.ds(0, n_chip - 1)], s_ret.at[e, g], r_ret.at[e, g]).wait_send()
            bulk(sib.at[e, g], s_sib.at[e, g], r_sib.at[e, g]).wait_send()
            bulk(oth.at[e, g], s_sib2.at[e, g], r_sib2.at[e, g]).wait_send()
        bulk(wsib.at[g], s_ws.at[g], r_ws.at[g]).wait_send()
        for i, h in enumerate(members(g)):

            @pl.when(chip != h)
            def _():
                bulk(wpair.at[0, g, i], s_wg.at[g, i], r_wg).wait_send()

    bulk(zgat.at[pl.ds(0, n_dp - 1)], s_z, r_z).wait_send()
    for c in stores:
        c.wait()
    wg_out.wait()


def body(n_dp, q, k, v, g, w):
    _, tok, width = q.shape
    heads = width // HEAD
    groups = heads // PER
    rows = PER // 2 * HEAD
    piece = rows // (SIDE * SIDE)
    hw = HEAD // 2
    act = pltpu.VMEM((tok, width), BF)
    wide = pltpu.VMEM((tok, width), F32)
    dma = pltpu.SemaphoreType.DMA
    block = pltpu.VMEM((2, groups, rows, HEAD), F32)
    slots = pltpu.VMEM((2, groups, SIDE * SIDE, piece, HEAD), F32)
    scratch = (
        [act] * 4 + [pltpu.VMEM((width, HEAD), BF)]
        + [act] * 4 + [pltpu.VMEM((hw, HEAD), F32)]
        + [act, act, wide, wide, act, wide, act, wide, wide]
        + [pltpu.VMEM((2, width, HEAD), F32)] * 2
        + [block, block, slots, slots, block, block]
        + [
            pltpu.VMEM((width, HEAD), F32),
            pltpu.VMEM((groups, PER, hw, HEAD), F32),
            pltpu.VMEM((2, groups, PER, hw, HEAD), F32),
            pltpu.VMEM((SIDE * SIDE, hw, HEAD), F32),
            pltpu.VMEM((hw, HEAD), F32),
            pltpu.VMEM((n_dp, hw, HEAD), F32),
        ]
        + [dma((4,)), dma, dma((4,))]
        + [dma((2, groups))] * 8
        + [dma((groups,))] * 2 + [dma((groups, PER)), dma, dma, dma]
        + [pltpu.SemaphoreType.REGULAR] * 2
    )
    outs = [jax.ShapeDtypeStruct(q.shape, BF)] * 4 + [jax.ShapeDtypeStruct((hw, HEAD), F32)]
    hbm = pl.BlockSpec(memory_space=pl.ANY)
    limit = 63 * 1024 * 1024
    results = pl.pallas_call(
        functools.partial(kernel, n_dp, heads, tok),
        out_shape=outs,
        in_specs=[hbm] * 5,
        out_specs=[hbm] * 5,
        scratch_shapes=scratch,
        compiler_params=pltpu.CompilerParams(
            collective_id=0, has_side_effects=True, vmem_limit_bytes=limit
        ),
        cost_estimate=pl.CostEstimate(
            flops=40 * heads * HEAD**3, bytes_accessed=5 * 2**20, transcendentals=0
        ),
    )(q, k, v, g, w)
    return pl.pallas_call(
        write_out,
        out_shape=outs,
        in_specs=[hbm] * 5,
        out_specs=[hbm] * 5,
        scratch_shapes=[pltpu.VMEM(o.shape, o.dtype) for o in outs] + [dma((2, 5))],
        compiler_params=pltpu.CompilerParams(vmem_limit_bytes=limit),
    )(*results)


def solution(mesh):
    spec = P("dp", "ctx", None)
    return jax.shard_map(
        functools.partial(body, mesh.shape["dp"]),
        mesh=mesh,
        in_specs=(spec, spec, spec, spec, P()),
        out_specs=(spec, spec, spec, spec, P("ctx", None)),
        check_vma=False,
    )
```

```python
import functools

import jax
import jax.numpy as jnp
from jax import lax
from jax.experimental import pallas as pl
from jax.experimental.pallas import tpu as pltpu
from jax.sharding import PartitionSpec as P

HEAD = 128
ORDER = (
    "pk0", "pk1", "fs0", "pk2", "fs1", "pk3", "fs2", "fs3", "pq0", "pq1", "pq2", "pq3", "fl0",
    "fl1", "c00", "c01", "fl2", "c02", "fl3", "c03", "relay", "nu0", "nu1", "nu2", "nu3",
    "relayed", "bl0", "bl1", "c10", "bl2", "c11", "bl3", "c12", "c13", "bf0", "bf1", "bf2",
    "bf3",
)
EPS = 1e-05
SIDE = 4
GROUPS = 4
PER = 2
FAR_FIRST = sorted(
    [(x, y) for x in range(SIDE) for y in range(SIDE) if x or y],
    key=lambda d: -sum(min(s, SIDE - s) for s in d),
)
MESH = pl.DeviceIdType.MESH
BF = jnp.bfloat16
F32 = jnp.float32
K, V, Q, G = range(4)
ATT, DQ, DK, DV = range(4)


def dot(a, b, ca, cb):
    return lax.dot_general(a, b, (((ca,), (cb,)), ((), ())), preferred_element_type=F32)


def split(x):
    high = x.astype(BF)
    return high, (x - high.astype(F32)).astype(BF)


def phi(z):
    return jnp.where(z > 0.0, z + 1.0, jnp.exp(jnp.minimum(z, 0.0)))


def write_out(*refs):
    src, dst, mid, sems = refs[:5], refs[5:10], refs[10:15], refs[15]
    ins = [pltpu.make_async_copy(src[i], mid[i], sems.at[0, i]) for i in range(5)]
    outs = [pltpu.make_async_copy(mid[i], dst[i], sems.at[1, i]) for i in range(5)]
    for c in ins:
        c.start()
    for a, b in zip(ins, outs):
        a.wait()
        b.start()
    for c in outs:
        c.wait()


def kernel(
    n_dp, tok,
    q_hbm, k_hbm, v_hbm, g_hbm, w_hbm,
    att_hbm, dq_hbm, dk_hbm, dv_hbm, wg_hbm,
    raw, w_ref, res, wg_ref,
    loc, give, got, back, came,
    qf_ref, kf_ref, sct_ref, m_ref, sq_ref, sk_ref, nl_ref, dkl_ref, dvl_ref,
    state, pair, gat, pre, ret,
    wl_ref, wgat, zsrc, zgat,
    in_sem, w_sem, out_sem,
    s_in, r_in, s_back, r_back, s_gat, r_gat, s_ret, r_ret,
    s_wg, r_wg, s_z, r_z, near_sem, far_sem,
):
    dp = lax.axis_index("dp")
    ctx = lax.axis_index("ctx")
    core = lax.rem(ctx, 2)
    chip = lax.div(ctx, 2)
    cx, cy = lax.div(chip, SIDE), lax.rem(chip, SIDE)
    near = (dp, ctx + 1 - 2 * core)
    n_chip = SIDE * SIDE
    rows = PER * HEAD
    piece = rows // n_chip
    hw = HEAD // 2

    def plane(dx, dy):
        o = lax.rem(cx + dx, SIDE) * SIDE + lax.rem(cy + dy, SIDE)
        return o, (dp, o * 2 + core)

    def zline(d):
        return (lax.rem(dp + d, n_dp), ctx)

    def remote(src, dst, ssem, rsem, where):
        return pltpu.make_async_remote_copy(
            src_ref=src, dst_ref=dst, send_sem=ssem, recv_sem=rsem,
            device_id=where, device_id_type=MESH,
        )

    def bulk(buf, ssem, rsem):
        return remote(buf, buf, ssem, rsem, near)

    def head(c, g, i):
        n = 2 * c + i
        return SIDE * n + lax.rem(n + g, SIDE)

    def cols(h):
        return pl.ds(pl.multiple_of(h * HEAD, HEAD), HEAD)

    def place(g, i):
        return pl.ds((g * PER + i) * HEAD, HEAD)

    w_load = pltpu.make_async_copy(w_hbm, w_ref, w_sem)
    loads = [
        pltpu.make_async_copy(src.at[0], raw.at[a], in_sem.at[a])
        for a, src in ((K, k_hbm), (V, v_hbm), (Q, q_hbm), (G, g_hbm))
    ]
    loads[K].start()
    loads[V].start()
    w_load.start()

    barrier = pltpu.get_barrier_semaphore()

    def greet(sem, where):
        pl.semaphore_signal(sem, inc=1, device_id=where, device_id_type=MESH)

    for d in FAR_FIRST:
        greet(barrier, plane(*d)[1])
    greet(barrier, near)
    greet(barrier, zline(1))
    greet(barrier, zline(n_dp - 1))

    def enter():
        loads[Q].start()
        loads[G].start()
        pl.semaphore_wait(barrier, 1 + len(FAR_FIRST) + 2)
        greet(near_sem, zline(1))
        greet(near_sem, zline(n_dp - 1))

    def relay():
        pl.semaphore_wait(near_sem, 2)
        greet(far_sem, zline(2))
        greet(far_sem, zline(n_dp - 2))

    def relayed():
        pl.semaphore_wait(far_sem, 2)

    rowid = lax.broadcasted_iota(jnp.int32, (tok, tok), 0)
    colid = lax.broadcasted_iota(jnp.int32, (tok, tok), 1)
    causal = rowid >= colid
    causal_t = rowid <= colid

    def lockstep(g, body):
        running = [body(g, i, b) for i in range(PER) for b in range(2)]
        while running:
            alive = []
            for r in running:
                try:
                    next(r)
                    alive.append(r)
                except StopIteration:
                    pass
            running = alive

    def pack(a, g):
        for i in range(PER):
            give[a, g, i] = raw[a, :, cols(head(1 - core, g, i))].astype(F32)
        remote(give.at[a, g], got.at[a, g], s_in.at[a, g], r_in.at[a, g], near).start()

    def keep(a, g):
        for i in range(PER):
            loc[a, 0, :, place(g, i)] = raw[a, :, cols(head(core, g, i))]

    def unpack(a, g):
        bulk(got.at[a, g], s_in.at[a, g], r_in.at[a, g]).wait_recv()
        for i in range(PER):
            loc[a, 1, :, place(g, i)] = got[a, g, i].astype(BF)

    def emit(o, g, i, b, value):
        if b == 0:
            res[o, :, cols(head(core, g, i))] = value.astype(BF)
        else:
            back[o, g, i] = value

    def send_back(o, g):
        remote(back.at[o, g], came.at[o, g], s_back.at[o, g], r_back.at[o, g], near).start()

    def take_back(o, g):
        bulk(came.at[o, g], s_back.at[o, g], r_back.at[o, g]).wait_recv()
        for i in range(PER):
            res[o, :, cols(head(1 - core, g, i))] = came[o, g, i].astype(BF)

    def weight(g, i):
        return w_ref[cols(head(core, g, i)), :]

    def outside(e, g, i, b):
        use = (core == 1) if e == b else (core == 0)
        other = state[e, 1 - b, place(g, i), :]
        return ret[e, g, pl.ds(i * HEAD, HEAD), :] + jnp.where(use, other, 0.0)

    def forward_state(g, i, b):
        c = place(g, i)
        z = dot(loc[K, b, :, c], weight(g, i), 1, 0)
        yield
        f = phi(z)
        kf = f.astype(BF)
        kf_ref[b, :, c] = kf
        sk_ref[b, :, c] = jnp.minimum(f, 1.0)
        yield
        state[0, b, c, :] = dot(kf, loc[V, b, :, c], 0, 0)

    def forward_local(g, i, b):
        c = place(g, i)
        z = dot(loc[Q, b, :, c], weight(g, i), 1, 0)
        yield
        f = phi(z)
        qf = f.astype(BF)
        qf_ref[b, :, c] = qf
        sq_ref[b, :, c] = jnp.minimum(f, 1.0)
        yield
        kf = kf_ref[b, :, c]
        w = jnp.where(causal, dot(qf, kf, 1, 1), 0.0).astype(BF)
        sct_ref[b, :, c] = jnp.where(causal_t, dot(kf, qf, 1, 1), 0.0).astype(BF)
        yield
        nl_ref[b, :, c] = dot(w, loc[V, b, :, c], 1, 0)

    def numer(g, i, b):
        c = place(g, i)
        qf = qf_ref[b, :, c]
        ph, plo = split(outside(0, g, i, b))
        yield
        n = dot(qf, ph, 1, 0) + dot(qf, plo, 1, 0) + nl_ref[b, :, c]
        yield
        r = lax.rsqrt(jnp.mean(n * n, axis=-1, keepdims=True) + EPS)
        yield
        normed = n * r
        og = loc[G, b, :, c].astype(F32)
        s = jnp.mean(og * normed, axis=-1, keepdims=True)
        yield
        m = (r * (og - normed * s)).astype(BF)
        m_ref[b, :, c] = m
        yield
        state[1, b, c, :] = dot(qf, m, 0, 0)
        emit(ATT, g, i, b, normed)

    def back_local(g, i, b):
        c = place(g, i)
        m, qf, kf, v = m_ref[b, :, c], qf_ref[b, :, c], kf_ref[b, :, c], loc[V, b, :, c]
        ph, plo = split(outside(0, g, i, b))
        s = jnp.where(causal, dot(m, v, 1, 1), 0.0).astype(BF)
        st = jnp.where(causal_t, dot(v, m, 1, 1), 0.0).astype(BF)
        yield
        qg = dot(m, ph, 1, 1) + dot(m, plo, 1, 1) + dot(s, kf, 1, 0)
        dkl_ref[b, :, c] = dot(st, qf, 1, 0)
        dvl_ref[b, :, c] = dot(sct_ref[b, :, c], m, 1, 0)
        yield
        qp = (qg * sq_ref[b, :, c]).astype(BF)
        yield
        wl_ref[b, c, :] = dot(loc[Q, b, :, c], qp, 0, 0)
        emit(DQ, g, i, b, dot(qp, weight(g, i), 1, 1))

    def back_final(g, i, b):
        c = place(g, i)
        qh, ql = split(outside(1, g, i, b))
        v, kf = loc[V, b, :, c], kf_ref[b, :, c]
        yield
        kg = dot(v, qh, 1, 1) + dot(v, ql, 1, 1) + dkl_ref[b, :, c]
        yield
        kp = (kg * sk_ref[b, :, c]).astype(BF)
        yield
        wl_ref[b, c, :] += dot(loc[K, b, :, c], kp, 0, 0)
        yield
        dv = dot(kf, qh, 1, 0) + dot(kf, ql, 1, 0) + dvl_ref[b, :, c]
        dk = dot(kp, weight(g, i), 1, 1)
        yield
        emit(DV, g, i, b, dv)
        emit(DK, g, i, b, dk)

    def part(o):
        return pl.ds(pl.multiple_of(o * piece, piece), piece)

    def scan_gather(e, g):
        c = pl.ds(g * rows, rows)
        pair[e, g] = state[e, 0, c, :] + state[e, 1, c, :]
        for d in FAR_FIRST:
            o, where = plane(*d)
            remote(
                pair.at[e, g, part(o), :], gat.at[e, g, chip],
                s_gat.at[e, g], r_gat.at[e, g], where,
            ).start()
        gat[e, g, chip] = pair[e, g, part(chip), :]

    def scan_return(e, g):
        bulk(gat.at[e, g, pl.ds(0, n_chip - 1)], s_gat.at[e, g], r_gat.at[e, g]).wait_recv()
        order = range(n_chip) if e == 0 else range(n_chip - 1, -1, -1)
        total = jnp.zeros((piece, HEAD), F32)
        for p in order:
            pre[e, g, p] = total
            total = total + gat[e, g, p]
        for d in FAR_FIRST:
            o, where = plane(*d)
            remote(
                pre.at[e, g, o], ret.at[e, g, part(chip), :],
                s_ret.at[e, g], r_ret.at[e, g], where,
            ).start()
        ret[e, g, part(chip), :] = pre[e, g, chip]

    def scan_wait(e, g):
        bulk(
            ret.at[e, g, pl.ds(0, rows - piece), :], s_ret.at[e, g], r_ret.at[e, g]
        ).wait_recv()

    def weight_parts(g):
        for i in range(PER):
            h = head(core, g, i)
            for c in range(2):
                yield i, c, (dp, 2 * h + c), (chip == h) & (core == c)

    def weight_send(g):
        for i in range(PER):
            wl_ref[0, place(g, i), :] += wl_ref[1, place(g, i), :]
        for i, c, where, own in weight_parts(g):
            part_rows = pl.ds((g * PER + i) * HEAD + c * hw, hw)

            @pl.when(jnp.logical_not(own))
            def _():
                remote(
                    wl_ref.at[0, part_rows, :], wgat.at[chip], s_wg.at[g, i, c], r_wg, where
                ).start()

            @pl.when(own)
            def _():
                wgat[chip] = wl_ref[0, part_rows, :]

    def weight_sum():
        own = core == lax.div(chip, n_chip // 2)

        @pl.when(own)
        def _():
            bulk(wgat.at[pl.ds(0, n_chip - 1)], s_z, r_wg).wait_recv()

        @pl.when(jnp.logical_not(own))
        def _():
            bulk(wgat, s_z, r_wg).wait_recv()

        total = wgat[0]
        for p in range(1, n_chip):
            total = total + wgat[p]
        zsrc[...] = total
        for d in (4, 3, 5, 2, 6, 1, 7):
            remote(zsrc, zgat.at[dp], s_z, r_z, zline(d)).start()
        zgat[dp] = total

    def weight_finish():
        bulk(zgat.at[pl.ds(0, n_dp - 1)], s_z, r_z).wait_recv()
        total = zgat[0]
        for z in range(1, n_dp):
            total = total + zgat[z]
        wg_ref[...] = total

    stores = []

    def store(o, dst):
        c = pltpu.make_async_copy(res.at[o], dst.at[0], out_sem.at[o])
        c.start()
        stores.append(c)

    first = [False] * 3

    def once(i, action):
        if not first[i]:
            first[i] = True
            action()

    def step(name, g):
        if name == "pk":
            once(0, lambda: (loads[K].wait(), loads[V].wait(), enter()))
            pack(K, g)
            pack(V, g)
        elif name == "fs":
            once(1, lambda: w_load.wait())
            keep(K, g)
            keep(V, g)
            unpack(K, g)
            unpack(V, g)
            lockstep(g, forward_state)
            scan_gather(0, g)
        elif name == "pq":
            once(2, lambda: (loads[Q].wait(), loads[G].wait()))
            pack(Q, g)
            pack(G, g)
            keep(Q, g)
            keep(G, g)
        elif name == "fl":
            unpack(Q, g)
            unpack(G, g)
            lockstep(g, forward_local)
        elif name == "c0":
            scan_return(0, g)
        elif name == "nu":
            scan_wait(0, g)
            lockstep(g, numer)
            scan_gather(1, g)
            send_back(ATT, g)
        elif name == "bl":
            lockstep(g, back_local)
            send_back(DQ, g)
        elif name == "c1":
            scan_return(1, g)
        elif name == "bf":
            scan_wait(1, g)
            lockstep(g, back_final)
            weight_send(g)
            send_back(DK, g)
            send_back(DV, g)

    for word in ORDER:
        if word == "relay":
            relay()
        elif word == "relayed":
            relayed()
        else:
            step(word[:-1], int(word[-1]))
    for g in range(GROUPS):
        take_back(ATT, g)
        take_back(DQ, g)
    store(ATT, att_hbm)
    store(DQ, dq_hbm)
    weight_sum()
    for g in range(GROUPS):
        take_back(DK, g)
        take_back(DV, g)
    store(DK, dk_hbm)
    store(DV, dv_hbm)
    weight_finish()
    wg_out = pltpu.make_async_copy(wg_ref, wg_hbm, w_sem)
    wg_out.start()

    for g in range(GROUPS):
        for a in range(4):
            bulk(give.at[a, g], s_in.at[a, g], r_in.at[a, g]).wait_send()
            bulk(back.at[a, g], s_back.at[a, g], r_back.at[a, g]).wait_send()
        for e in range(2):
            bulk(gat.at[e, g, pl.ds(0, n_chip - 1)], s_gat.at[e, g], r_gat.at[e, g]).wait_send()
            bulk(pre.at[e, g, pl.ds(0, n_chip - 1)], s_ret.at[e, g], r_ret.at[e, g]).wait_send()
        for i, c, where, own in weight_parts(g):

            @pl.when(jnp.logical_not(own))
            def _():
                bulk(zsrc, s_wg.at[g, i, c], r_wg).wait_send()

    bulk(zgat.at[pl.ds(0, n_dp - 1)], s_z, r_z).wait_send()
    for c in stores:
        c.wait()
    wg_out.wait()


def body(n_dp, q, k, v, g, w):
    _, tok, width = q.shape
    mine = GROUPS * PER * HEAD
    rows = PER * HEAD
    n_chip = SIDE * SIDE
    hw = HEAD // 2
    dma = pltpu.SemaphoreType.DMA
    act = pltpu.VMEM((2, tok, mine), BF)
    wide = pltpu.VMEM((2, tok, mine), F32)
    moved = pltpu.VMEM((4, GROUPS, PER, tok, HEAD), F32)
    block = pltpu.VMEM((2, GROUPS, rows, HEAD), F32)
    slots = pltpu.VMEM((2, GROUPS, n_chip, rows // n_chip, HEAD), F32)
    part = pltpu.VMEM((hw, HEAD), F32)
    scratch = (
        [pltpu.VMEM((4, tok, width), BF), pltpu.VMEM((width, HEAD), BF)]
        + [pltpu.VMEM((4, tok, width), BF), part]
        + [pltpu.VMEM((4, 2, tok, mine), BF)] + [moved] * 4
        + [act] * 4 + [wide] * 5
        + [pltpu.VMEM((2, 2, mine, HEAD), F32), block, slots, slots, block]
        + [pltpu.VMEM((2, mine, HEAD), F32), pltpu.VMEM((n_chip, hw, HEAD), F32)]
        + [part, pltpu.VMEM((n_dp, hw, HEAD), F32)]
        + [dma((4,)), dma, dma((4,))]
        + [dma((4, GROUPS))] * 4 + [dma((2, GROUPS))] * 4
        + [dma((GROUPS, PER, 2)), dma, dma, dma]
        + [pltpu.SemaphoreType.REGULAR] * 2
    )
    outs = [jax.ShapeDtypeStruct(q.shape, BF)] * 4 + [jax.ShapeDtypeStruct((hw, HEAD), F32)]
    hbm = pl.BlockSpec(memory_space=pl.ANY)
    limit = 63 * 1024 * 1024
    results = pl.pallas_call(
        functools.partial(kernel, n_dp, tok),
        out_shape=outs,
        in_specs=[hbm] * 5,
        out_specs=[hbm] * 5,
        scratch_shapes=scratch,
        compiler_params=pltpu.CompilerParams(
            collective_id=0, has_side_effects=True, vmem_limit_bytes=limit
        ),
        cost_estimate=pl.CostEstimate(
            flops=80 * mine * HEAD**2, bytes_accessed=5 * 2**20, transcendentals=0
        ),
    )(q, k, v, g, w)
    return pl.pallas_call(
        write_out,
        out_shape=outs,
        in_specs=[hbm] * 5,
        out_specs=[hbm] * 5,
        scratch_shapes=[pltpu.VMEM(o.shape, o.dtype) for o in outs] + [dma((2, 5))],
        compiler_params=pltpu.CompilerParams(vmem_limit_bytes=limit),
    )(*results)


def solution(mesh):
    spec = P("dp", "ctx", None)
    return jax.shard_map(
        functools.partial(body, mesh.shape["dp"]),
        mesh=mesh,
        in_specs=(spec, spec, spec, spec, P()),
        out_specs=(spec, spec, spec, spec, P("ctx", None)),
        check_vma=False,
    )
```

```python
import functools

import jax
import jax.numpy as jnp
from jax import lax
from jax.experimental import pallas as pl
from jax.experimental.pallas import tpu as pltpu
from jax.sharding import PartitionSpec as P

HEAD = 128
ORDER = (
    "fs0", "fs1", "fs2", "fs3", "ss0", "ss1", "ss2", "ss3", "gs0", "gs1", "gs2", "gs3", "pk0",
    "pk1", "pq0", "pq1", "pk2", "pk3", "pq2", "pq3", "kf0", "fl0", "kf1", "fl1", "c00", "c01",
    "kf2", "fl2", "c02", "kf3", "fl3", "c03", "relay", "nu0", "nu1", "nu2", "nu3", "relayed",
    "bl0", "bl1", "c10", "bl2", "c11", "bl3", "c12", "c13", "bf0", "bf1", "bf2", "bf3",
)
EPS = 1e-05
SIDE = 4
GROUPS = 4
PER = 2
FAR_FIRST = sorted(
    [(x, y) for x in range(SIDE) for y in range(SIDE) if x or y],
    key=lambda d: -sum(min(s, SIDE - s) for s in d),
)
MESH = pl.DeviceIdType.MESH
BF = jnp.bfloat16
F32 = jnp.float32
K, V, Q, G = range(4)
ATT, DQ, DK, DV = range(4)


def dot(a, b, ca, cb):
    return lax.dot_general(a, b, (((ca,), (cb,)), ((), ())), preferred_element_type=F32)


def split(x):
    high = x.astype(BF)
    return high, (x - high.astype(F32)).astype(BF)


def phi(z):
    return jnp.where(z > 0.0, z + 1.0, jnp.exp(jnp.minimum(z, 0.0)))


def write_out(*refs):
    src, dst, mid, sems = refs[:5], refs[5:10], refs[10:15], refs[15]
    ins = [pltpu.make_async_copy(src[i], mid[i], sems.at[0, i]) for i in range(5)]
    outs = [pltpu.make_async_copy(mid[i], dst[i], sems.at[1, i]) for i in range(5)]
    for c in ins:
        c.start()
    for a, b in zip(ins, outs):
        a.wait()
        b.start()
    for c in outs:
        c.wait()


def kernel(
    n_dp, tok,
    q_hbm, k_hbm, v_hbm, g_hbm, w_hbm,
    att_hbm, dq_hbm, dk_hbm, dv_hbm, wg_hbm,
    raw, w_ref, res, wg_ref,
    loc, give, got, back, came,
    qf_ref, kf_ref, sct_ref, m_ref, sq_ref, sk_ref, nl_ref, dkl_ref, dvl_ref,
    state, lent, pair, gat, pre, ret,
    wl_ref, wgat, zsrc, zgat,
    in_sem, w_sem, out_sem,
    s_in, r_in, s_back, r_back, s_gat, r_gat, s_ret, r_ret,
    s_lent, r_lent, s_wg, r_wg, s_z, r_z, near_sem, far_sem,
):
    dp = lax.axis_index("dp")
    ctx = lax.axis_index("ctx")
    core = lax.rem(ctx, 2)
    chip = lax.div(ctx, 2)
    cx, cy = lax.div(chip, SIDE), lax.rem(chip, SIDE)
    near = (dp, ctx + 1 - 2 * core)
    n_chip = SIDE * SIDE
    rows = PER * HEAD
    piece = rows // n_chip
    hw = HEAD // 2

    def plane(dx, dy):
        o = lax.rem(cx + dx, SIDE) * SIDE + lax.rem(cy + dy, SIDE)
        return o, (dp, o * 2 + core)

    def zline(d):
        return (lax.rem(dp + d, n_dp), ctx)

    def remote(src, dst, ssem, rsem, where):
        return pltpu.make_async_remote_copy(
            src_ref=src, dst_ref=dst, send_sem=ssem, recv_sem=rsem,
            device_id=where, device_id_type=MESH,
        )

    def bulk(buf, ssem, rsem):
        return remote(buf, buf, ssem, rsem, near)

    def head(c, g, i):
        n = 2 * c + i
        return SIDE * n + lax.rem(n + g, SIDE)

    def cols(h):
        return pl.ds(pl.multiple_of(h * HEAD, HEAD), HEAD)

    def place(g, i):
        return pl.ds((g * PER + i) * HEAD, HEAD)

    w_load = pltpu.make_async_copy(w_hbm, w_ref, w_sem)
    loads = [
        pltpu.make_async_copy(src.at[0], raw.at[a], in_sem.at[a])
        for a, src in ((K, k_hbm), (V, v_hbm), (Q, q_hbm), (G, g_hbm))
    ]
    loads[K].start()
    loads[V].start()
    w_load.start()

    barrier = pltpu.get_barrier_semaphore()

    def greet(sem, where):
        pl.semaphore_signal(sem, inc=1, device_id=where, device_id_type=MESH)

    for d in FAR_FIRST:
        greet(barrier, plane(*d)[1])
    greet(barrier, near)
    greet(barrier, zline(1))
    greet(barrier, zline(n_dp - 1))

    def enter():
        loads[Q].start()
        loads[G].start()
        pl.semaphore_wait(barrier, 1 + len(FAR_FIRST) + 2)
        greet(near_sem, zline(1))
        greet(near_sem, zline(n_dp - 1))

    def relay():
        pl.semaphore_wait(near_sem, 2)
        greet(far_sem, zline(2))
        greet(far_sem, zline(n_dp - 2))

    def relayed():
        pl.semaphore_wait(far_sem, 2)

    rowid = lax.broadcasted_iota(jnp.int32, (tok, tok), 0)
    colid = lax.broadcasted_iota(jnp.int32, (tok, tok), 1)
    causal = rowid >= colid
    causal_t = rowid <= colid

    def lockstep(g, body, blocks=(0, 1)):
        running = [body(g, i, b) for i in range(PER) for b in blocks]
        while running:
            alive = []
            for r in running:
                try:
                    next(r)
                    alive.append(r)
                except StopIteration:
                    pass
            running = alive

    def pack(a, g):
        for i in range(PER):
            give[a, g, i] = raw[a, :, cols(head(1 - core, g, i))].astype(F32)
        remote(give.at[a, g], got.at[a, g], s_in.at[a, g], r_in.at[a, g], near).start()

    def keep(a, g):
        for i in range(PER):
            loc[a, 0, :, place(g, i)] = raw[a, :, cols(head(core, g, i))]

    def unpack(a, g):
        bulk(got.at[a, g], s_in.at[a, g], r_in.at[a, g]).wait_recv()
        for i in range(PER):
            loc[a, 1, :, place(g, i)] = got[a, g, i].astype(BF)

    def emit(o, g, i, b, value):
        if b == 0:
            res[o, :, cols(head(core, g, i))] = value.astype(BF)
        else:
            back[o, g, i] = value

    def send_back(o, g):
        remote(back.at[o, g], came.at[o, g], s_back.at[o, g], r_back.at[o, g], near).start()

    def take_back(o, g):
        bulk(came.at[o, g], s_back.at[o, g], r_back.at[o, g]).wait_recv()
        for i in range(PER):
            res[o, :, cols(head(1 - core, g, i))] = came[o, g, i].astype(BF)

    def weight(g, i):
        return w_ref[cols(head(core, g, i)), :]

    def outside(e, g, i, b):
        use = (core == 1) if e == b else (core == 0)
        other = state[e, 1 - b, place(g, i), :]
        return ret[e, g, pl.ds(i * HEAD, HEAD), :] + jnp.where(use, other, 0.0)

    def key_side(g, i, b):
        c = place(g, i)
        z = dot(loc[K, b, :, c], weight(g, i), 1, 0)
        yield
        f = phi(z)
        kf_ref[b, :, c] = f.astype(BF)
        sk_ref[b, :, c] = jnp.minimum(f, 1.0)

    def forward_state(g, i, own):
        c = cols(head(core if own else 1 - core, g, i))
        z = dot(raw[K, :, c], w_ref[c, :], 1, 0)
        yield
        f = phi(z)
        kf = f.astype(BF)
        if own:
            kf_ref[0, :, place(g, i)] = kf
            sk_ref[0, :, place(g, i)] = jnp.minimum(f, 1.0)
        yield
        s = dot(kf, raw[V, :, c], 0, 0)
        if own:
            state[0, 0, place(g, i), :] = s
        else:
            lent[g, pl.ds(i * HEAD, HEAD), :] = s

    def swap_state(g):
        return remote(
            lent.at[g], state.at[0, 1, pl.ds(g * rows, rows), :], s_lent.at[g], r_lent.at[g], near
        )

    def forward_local(g, i, b):
        c = place(g, i)
        z = dot(loc[Q, b, :, c], weight(g, i), 1, 0)
        yield
        f = phi(z)
        qf = f.astype(BF)
        qf_ref[b, :, c] = qf
        sq_ref[b, :, c] = jnp.minimum(f, 1.0)
        yield
        kf = kf_ref[b, :, c]
        w = jnp.where(causal, dot(qf, kf, 1, 1), 0.0).astype(BF)
        sct_ref[b, :, c] = jnp.where(causal_t, dot(kf, qf, 1, 1), 0.0).astype(BF)
        yield
        nl_ref[b, :, c] = dot(w, loc[V, b, :, c], 1, 0)

    def numer(g, i, b):
        c = place(g, i)
        qf = qf_ref[b, :, c]
        ph, plo = split(outside(0, g, i, b))
        yield
        n = dot(qf, ph, 1, 0) + dot(qf, plo, 1, 0) + nl_ref[b, :, c]
        yield
        r = lax.rsqrt(jnp.mean(n * n, axis=-1, keepdims=True) + EPS)
        yield
        normed = n * r
        og = loc[G, b, :, c].astype(F32)
        s = jnp.mean(og * normed, axis=-1, keepdims=True)
        yield
        m = (r * (og - normed * s)).astype(BF)
        m_ref[b, :, c] = m
        yield
        state[1, b, c, :] = dot(qf, m, 0, 0)
        emit(ATT, g, i, b, normed)

    def back_local(g, i, b):
        c = place(g, i)
        m, qf, kf, v = m_ref[b, :, c], qf_ref[b, :, c], kf_ref[b, :, c], loc[V, b, :, c]
        ph, plo = split(outside(0, g, i, b))
        s = jnp.where(causal, dot(m, v, 1, 1), 0.0).astype(BF)
        st = jnp.where(causal_t, dot(v, m, 1, 1), 0.0).astype(BF)
        yield
        qg = dot(m, ph, 1, 1) + dot(m, plo, 1, 1) + dot(s, kf, 1, 0)
        dkl_ref[b, :, c] = dot(st, qf, 1, 0)
        dvl_ref[b, :, c] = dot(sct_ref[b, :, c], m, 1, 0)
        yield
        qp = (qg * sq_ref[b, :, c]).astype(BF)
        yield
        wl_ref[b, c, :] = dot(loc[Q, b, :, c], qp, 0, 0)
        emit(DQ, g, i, b, dot(qp, weight(g, i), 1, 1))

    def back_final(g, i, b):
        c = place(g, i)
        qh, ql = split(outside(1, g, i, b))
        v, kf = loc[V, b, :, c], kf_ref[b, :, c]
        yield
        kg = dot(v, qh, 1, 1) + dot(v, ql, 1, 1) + dkl_ref[b, :, c]
        yield
        kp = (kg * sk_ref[b, :, c]).astype(BF)
        yield
        wl_ref[b, c, :] += dot(loc[K, b, :, c], kp, 0, 0)
        yield
        dv = dot(kf, qh, 1, 0) + dot(kf, ql, 1, 0) + dvl_ref[b, :, c]
        dk = dot(kp, weight(g, i), 1, 1)
        yield
        emit(DV, g, i, b, dv)
        emit(DK, g, i, b, dk)

    def part(o):
        return pl.ds(pl.multiple_of(o * piece, piece), piece)

    def scan_gather(e, g):
        c = pl.ds(g * rows, rows)
        pair[e, g] = state[e, 0, c, :] + state[e, 1, c, :]
        for d in FAR_FIRST:
            o, where = plane(*d)
            remote(
                pair.at[e, g, part(o), :], gat.at[e, g, chip],
                s_gat.at[e, g], r_gat.at[e, g], where,
            ).start()
        gat[e, g, chip] = pair[e, g, part(chip), :]

    def scan_return(e, g):
        bulk(gat.at[e, g, pl.ds(0, n_chip - 1)], s_gat.at[e, g], r_gat.at[e, g]).wait_recv()
        order = range(n_chip) if e == 0 else range(n_chip - 1, -1, -1)
        total = jnp.zeros((piece, HEAD), F32)
        for p in order:
            pre[e, g, p] = total
            total = total + gat[e, g, p]
        for d in FAR_FIRST:
            o, where = plane(*d)
            remote(
                pre.at[e, g, o], ret.at[e, g, part(chip), :],
                s_ret.at[e, g], r_ret.at[e, g], where,
            ).start()
        ret[e, g, part(chip), :] = pre[e, g, chip]

    def scan_wait(e, g):
        bulk(
            ret.at[e, g, pl.ds(0, rows - piece), :], s_ret.at[e, g], r_ret.at[e, g]
        ).wait_recv()

    def weight_parts(g):
        for i in range(PER):
            h = head(core, g, i)
            for c in range(2):
                yield i, c, (dp, 2 * h + c), (chip == h) & (core == c)

    def weight_send(g):
        for i in range(PER):
            wl_ref[0, place(g, i), :] += wl_ref[1, place(g, i), :]
        for i, c, where, own in weight_parts(g):
            part_rows = pl.ds((g * PER + i) * HEAD + c * hw, hw)

            @pl.when(jnp.logical_not(own))
            def _():
                remote(
                    wl_ref.at[0, part_rows, :], wgat.at[chip], s_wg.at[g, i, c], r_wg, where
                ).start()

            @pl.when(own)
            def _():
                wgat[chip] = wl_ref[0, part_rows, :]

    def weight_sum():
        own = core == lax.div(chip, n_chip // 2)

        @pl.when(own)
        def _():
            bulk(wgat.at[pl.ds(0, n_chip - 1)], s_z, r_wg).wait_recv()

        @pl.when(jnp.logical_not(own))
        def _():
            bulk(wgat, s_z, r_wg).wait_recv()

        total = wgat[0]
        for p in range(1, n_chip):
            total = total + wgat[p]
        zsrc[...] = total
        for z in range(n_dp):

            @pl.when(z != dp)
            def _():
                remote(zsrc, zgat.at[dp], s_z, r_z, (z, ctx)).start()

        zgat[dp] = total

    def weight_finish():
        bulk(zgat.at[pl.ds(0, n_dp - 1)], s_z, r_z).wait_recv()
        total = zgat[0]
        for z in range(1, n_dp):
            total = total + zgat[z]
        wg_ref[...] = total

    stores = []

    def store(o, dst):
        c = pltpu.make_async_copy(res.at[o], dst.at[0], out_sem.at[o])
        c.start()
        stores.append(c)

    first = [False] * 3

    def once(i, action):
        if not first[i]:
            first[i] = True
            action()

    def step(name, g):
        if name == "fs":
            once(0, lambda: (loads[K].wait(), loads[V].wait(), w_load.wait()))
            lockstep(g, forward_state, (True, False))
        elif name == "ss":
            once(1, enter)
            swap_state(g).start()
        elif name == "gs":
            swap_state(g).wait_recv()
            scan_gather(0, g)
        elif name == "pk":
            pack(K, g)
            pack(V, g)
            keep(K, g)
            keep(V, g)
        elif name == "pq":
            once(2, lambda: (loads[Q].wait(), loads[G].wait()))
            pack(Q, g)
            pack(G, g)
            keep(Q, g)
            keep(G, g)
        elif name == "kf":
            unpack(K, g)
            unpack(V, g)
            lockstep(g, key_side, (1,))
        elif name == "fl":
            unpack(Q, g)
            unpack(G, g)
            lockstep(g, forward_local)
        elif name == "c0":
            scan_return(0, g)
        elif name == "nu":
            scan_wait(0, g)
            lockstep(g, numer)
            scan_gather(1, g)
            send_back(ATT, g)
        elif name == "bl":
            lockstep(g, back_local)
            send_back(DQ, g)
        elif name == "c1":
            scan_return(1, g)
        elif name == "bf":
            scan_wait(1, g)
            lockstep(g, back_final)
            weight_send(g)
            send_back(DK, g)
            send_back(DV, g)

    for word in ORDER:
        if word == "relay":
            relay()
        elif word == "relayed":
            relayed()
        else:
            step(word[:-1], int(word[-1]))
    for g in range(GROUPS):
        take_back(ATT, g)
        take_back(DQ, g)
    store(ATT, att_hbm)
    store(DQ, dq_hbm)
    weight_sum()
    for g in range(GROUPS):
        take_back(DK, g)
        take_back(DV, g)
    store(DK, dk_hbm)
    store(DV, dv_hbm)
    weight_finish()
    wg_out = pltpu.make_async_copy(wg_ref, wg_hbm, w_sem)
    wg_out.start()

    for g in range(GROUPS):
        swap_state(g).wait_send()
        for a in range(4):
            bulk(give.at[a, g], s_in.at[a, g], r_in.at[a, g]).wait_send()
            bulk(back.at[a, g], s_back.at[a, g], r_back.at[a, g]).wait_send()
        for e in range(2):
            bulk(gat.at[e, g, pl.ds(0, n_chip - 1)], s_gat.at[e, g], r_gat.at[e, g]).wait_send()
            bulk(pre.at[e, g, pl.ds(0, n_chip - 1)], s_ret.at[e, g], r_ret.at[e, g]).wait_send()
        for i, c, where, own in weight_parts(g):

            @pl.when(jnp.logical_not(own))
            def _():
                bulk(zsrc, s_wg.at[g, i, c], r_wg).wait_send()

    bulk(zgat.at[pl.ds(0, n_dp - 1)], s_z, r_z).wait_send()
    for c in stores:
        c.wait()
    wg_out.wait()


def body(n_dp, q, k, v, g, w):
    _, tok, width = q.shape
    mine = GROUPS * PER * HEAD
    rows = PER * HEAD
    n_chip = SIDE * SIDE
    hw = HEAD // 2
    dma = pltpu.SemaphoreType.DMA
    act = pltpu.VMEM((2, tok, mine), BF)
    wide = pltpu.VMEM((2, tok, mine), F32)
    moved = pltpu.VMEM((4, GROUPS, PER, tok, HEAD), F32)
    block = pltpu.VMEM((2, GROUPS, rows, HEAD), F32)
    slots = pltpu.VMEM((2, GROUPS, n_chip, rows // n_chip, HEAD), F32)
    part = pltpu.VMEM((hw, HEAD), F32)
    scratch = (
        [pltpu.VMEM((4, tok, width), BF), pltpu.VMEM((width, HEAD), BF)]
        + [pltpu.VMEM((4, tok, width), BF), part]
        + [pltpu.VMEM((4, 2, tok, mine), BF)] + [moved] * 4
        + [act] * 4 + [wide] * 5
        + [pltpu.VMEM((2, 2, mine, HEAD), F32), pltpu.VMEM((GROUPS, rows, HEAD), F32), block, slots, slots, block]
        + [pltpu.VMEM((2, mine, HEAD), F32), pltpu.VMEM((n_chip, hw, HEAD), F32)]
        + [part, pltpu.VMEM((n_dp, hw, HEAD), F32)]
        + [dma((4,)), dma, dma((4,))]
        + [dma((4, GROUPS))] * 4 + [dma((2, GROUPS))] * 4
        + [dma((GROUPS,))] * 2 + [dma((GROUPS, PER, 2)), dma, dma, dma]
        + [pltpu.SemaphoreType.REGULAR] * 2
    )
    outs = [jax.ShapeDtypeStruct(q.shape, BF)] * 4 + [jax.ShapeDtypeStruct((hw, HEAD), F32)]
    hbm = pl.BlockSpec(memory_space=pl.ANY)
    limit = 63 * 1024 * 1024
    results = pl.pallas_call(
        functools.partial(kernel, n_dp, tok),
        out_shape=outs,
        in_specs=[hbm] * 5,
        out_specs=[hbm] * 5,
        scratch_shapes=scratch,
        compiler_params=pltpu.CompilerParams(
            collective_id=0, has_side_effects=True, vmem_limit_bytes=limit
        ),
        cost_estimate=pl.CostEstimate(
            flops=80 * mine * HEAD**2, bytes_accessed=5 * 2**20, transcendentals=0
        ),
    )(q, k, v, g, w)
    return pl.pallas_call(
        write_out,
        out_shape=outs,
        in_specs=[hbm] * 5,
        out_specs=[hbm] * 5,
        scratch_shapes=[pltpu.VMEM(o.shape, o.dtype) for o in outs] + [dma((2, 5))],
        compiler_params=pltpu.CompilerParams(vmem_limit_bytes=limit),
    )(*results)


def solution(mesh):
    spec = P("dp", "ctx", None)
    return jax.shard_map(
        functools.partial(body, mesh.shape["dp"]),
        mesh=mesh,
        in_specs=(spec, spec, spec, spec, P()),
        out_specs=(spec, spec, spec, spec, P("ctx", None)),
        check_vma=False,
    )
```

```python
import functools

import jax
import jax.numpy as jnp
from jax import lax
from jax.experimental import pallas as pl
from jax.experimental.pallas import tpu as pltpu
from jax.sharding import PartitionSpec as P

HEAD = 128
ORDER = (
    "fs0", "fs1", "fs2", "fs3", "ss0", "ss1", "ss2", "ss3", "gs0", "gs1", "gs2", "gs3", "pk0",
    "pk1", "pq0", "pq1", "pk2", "pk3", "pq2", "pq3", "kf0", "fl0", "kf1", "c00", "fl1", "c01",
    "kf2", "c02", "fl2", "c03", "kf3", "fl3", "relay", "nu0", "nu1", "nu2", "nu3", "relayed",
    "bl0", "c10", "bl1", "c11", "bl2", "c12", "bl3", "c13", "bf0", "bf1", "bf2", "bf3", "br0",
    "br1", "br2", "br3",
)
EPS = 1e-05
SIDE = 4
GROUPS = 4
PER = 2
FAR_FIRST = sorted(
    [(x, y) for x in range(SIDE) for y in range(SIDE) if x or y],
    key=lambda d: -sum(min(s, SIDE - s) for s in d),
)
MESH = pl.DeviceIdType.MESH
BF = jnp.bfloat16
F32 = jnp.float32
K, V, Q, G = range(4)
ATT, DQ, DK, DV = range(4)


def dot(a, b, ca, cb):
    return lax.dot_general(a, b, (((ca,), (cb,)), ((), ())), preferred_element_type=F32)


def split(x):
    high = x.astype(BF)
    return high, (x - high.astype(F32)).astype(BF)


def phi(z):
    return jnp.where(z > 0.0, z + 1.0, jnp.exp(jnp.minimum(z, 0.0)))


def write_out(*refs):
    src, dst, mid, sems = refs[:5], refs[5:10], refs[10:15], refs[15]
    ins = [pltpu.make_async_copy(src[i], mid[i], sems.at[0, i]) for i in range(5)]
    outs = [pltpu.make_async_copy(mid[i], dst[i], sems.at[1, i]) for i in range(5)]
    for c in ins:
        c.start()
    for a, b in zip(ins, outs):
        a.wait()
        b.start()
    for c in outs:
        c.wait()


def kernel(
    n_dp, tok,
    q_hbm, k_hbm, v_hbm, g_hbm, w_hbm,
    att_hbm, dq_hbm, dk_hbm, dv_hbm, wg_hbm,
    raw, w_ref, res, wg_ref,
    loc, give, got, back, came,
    qf_ref, kf_ref, sct_ref, m_ref, kp_ref, sq_ref, sk_ref, nl_ref, dkl_ref, dvl_ref,
    state, lent, pair, gat, pre, ret,
    wl_ref, wgat, zsrc, zgat,
    in_sem, w_sem, out_sem,
    s_in, r_in, s_back, r_back, s_gat, r_gat, s_ret, r_ret,
    s_lent, r_lent, s_wg, r_wg, s_z, r_z, near_sem, far_sem,
):
    dp = lax.axis_index("dp")
    ctx = lax.axis_index("ctx")
    core = lax.rem(ctx, 2)
    chip = lax.div(ctx, 2)
    cx, cy = lax.div(chip, SIDE), lax.rem(chip, SIDE)
    near = (dp, ctx + 1 - 2 * core)
    n_chip = SIDE * SIDE
    rows = PER * HEAD
    piece = rows // n_chip
    hw = HEAD // 2

    def plane(dx, dy):
        o = lax.rem(cx + dx, SIDE) * SIDE + lax.rem(cy + dy, SIDE)
        return o, (dp, o * 2 + core)

    def zline(d):
        return (lax.rem(dp + d, n_dp), ctx)

    def remote(src, dst, ssem, rsem, where):
        return pltpu.make_async_remote_copy(
            src_ref=src, dst_ref=dst, send_sem=ssem, recv_sem=rsem,
            device_id=where, device_id_type=MESH,
        )

    def bulk(buf, ssem, rsem):
        return remote(buf, buf, ssem, rsem, near)

    def head(c, g, i):
        n = 2 * c + i
        return SIDE * n + lax.rem(n + g, SIDE)

    def cols(h):
        return pl.ds(pl.multiple_of(h * HEAD, HEAD), HEAD)

    def place(g, i):
        return pl.ds((g * PER + i) * HEAD, HEAD)

    w_load = pltpu.make_async_copy(w_hbm, w_ref, w_sem)
    loads = [
        pltpu.make_async_copy(src.at[0], raw.at[a], in_sem.at[a])
        for a, src in ((K, k_hbm), (V, v_hbm), (Q, q_hbm), (G, g_hbm))
    ]
    loads[K].start()
    loads[V].start()
    w_load.start()

    barrier = pltpu.get_barrier_semaphore()

    def greet(sem, where):
        pl.semaphore_signal(sem, inc=1, device_id=where, device_id_type=MESH)

    for d in FAR_FIRST:
        greet(barrier, plane(*d)[1])
    greet(barrier, near)
    greet(barrier, zline(1))
    greet(barrier, zline(n_dp - 1))

    def enter():
        loads[Q].start()
        loads[G].start()
        pl.semaphore_wait(barrier, 1 + len(FAR_FIRST) + 2)
        greet(near_sem, zline(1))
        greet(near_sem, zline(n_dp - 1))

    def relay():
        pl.semaphore_wait(near_sem, 2)
        greet(far_sem, zline(2))
        greet(far_sem, zline(n_dp - 2))

    def relayed():
        pl.semaphore_wait(far_sem, 2)

    rowid = lax.broadcasted_iota(jnp.int32, (tok, tok), 0)
    colid = lax.broadcasted_iota(jnp.int32, (tok, tok), 1)
    causal = rowid >= colid
    causal_t = rowid <= colid

    def lockstep(g, body, blocks=(0, 1)):
        running = [body(g, i, b) for i in range(PER) for b in blocks]
        while running:
            alive = []
            for r in running:
                try:
                    next(r)
                    alive.append(r)
                except StopIteration:
                    pass
            running = alive

    def pack(a, g):
        for i in range(PER):
            give[a, g, i] = raw[a, :, cols(head(1 - core, g, i))].astype(F32)
        remote(give.at[a, g], got.at[a, g], s_in.at[a, g], r_in.at[a, g], near).start()

    def keep(a, g):
        for i in range(PER):
            loc[a, 0, :, place(g, i)] = raw[a, :, cols(head(core, g, i))]

    def unpack(a, g):
        bulk(got.at[a, g], s_in.at[a, g], r_in.at[a, g]).wait_recv()
        for i in range(PER):
            loc[a, 1, :, place(g, i)] = got[a, g, i].astype(BF)

    def emit(o, g, i, b, value):
        if b == 0:
            res[o, :, cols(head(core, g, i))] = value.astype(BF)
        else:
            back[o, g, i] = value

    def send_back(o, g):
        remote(back.at[o, g], came.at[o, g], s_back.at[o, g], r_back.at[o, g], near).start()

    def take_back(o, g):
        bulk(came.at[o, g], s_back.at[o, g], r_back.at[o, g]).wait_recv()
        for i in range(PER):
            res[o, :, cols(head(1 - core, g, i))] = came[o, g, i].astype(BF)

    def weight(g, i):
        return w_ref[cols(head(core, g, i)), :]

    def outside(e, g, i, b):
        use = (core == 1) if e == b else (core == 0)
        other = state[e, 1 - b, place(g, i), :]
        return ret[e, g, pl.ds(i * HEAD, HEAD), :] + jnp.where(use, other, 0.0)

    def key_side(g, i, b):
        c = place(g, i)
        z = dot(loc[K, b, :, c], weight(g, i), 1, 0)
        yield
        f = phi(z)
        kf_ref[b, :, c] = f.astype(BF)
        sk_ref[b, :, c] = jnp.minimum(f, 1.0)

    def forward_state(g, i, own):
        c = cols(head(core if own else 1 - core, g, i))
        z = dot(raw[K, :, c], w_ref[c, :], 1, 0)
        yield
        f = phi(z)
        kf = f.astype(BF)
        if own:
            kf_ref[0, :, place(g, i)] = kf
            sk_ref[0, :, place(g, i)] = jnp.minimum(f, 1.0)
        yield
        s = dot(kf, raw[V, :, c], 0, 0)
        if own:
            state[0, 0, place(g, i), :] = s
        else:
            lent[g, pl.ds(i * HEAD, HEAD), :] = s

    def swap_state(g):
        return remote(
            lent.at[g], state.at[0, 1, pl.ds(g * rows, rows), :], s_lent.at[g], r_lent.at[g], near
        )

    def forward_local(g, i, b):
        c = place(g, i)
        z = dot(loc[Q, b, :, c], weight(g, i), 1, 0)
        yield
        f = phi(z)
        qf = f.astype(BF)
        qf_ref[b, :, c] = qf
        sq_ref[b, :, c] = jnp.minimum(f, 1.0)
        yield
        kf = kf_ref[b, :, c]
        w = jnp.where(causal, dot(qf, kf, 1, 1), 0.0).astype(BF)
        sct_ref[b, :, c] = jnp.where(causal_t, dot(kf, qf, 1, 1), 0.0).astype(BF)
        yield
        nl_ref[b, :, c] = dot(w, loc[V, b, :, c], 1, 0)

    def numer(g, i, b):
        c = place(g, i)
        qf = qf_ref[b, :, c]
        ph, plo = split(outside(0, g, i, b))
        yield
        n = dot(qf, ph, 1, 0) + dot(qf, plo, 1, 0) + nl_ref[b, :, c]
        yield
        r = lax.rsqrt(jnp.mean(n * n, axis=-1, keepdims=True) + EPS)
        yield
        normed = n * r
        og = loc[G, b, :, c].astype(F32)
        s = jnp.mean(og * normed, axis=-1, keepdims=True)
        yield
        m = (r * (og - normed * s)).astype(BF)
        m_ref[b, :, c] = m
        yield
        state[1, b, c, :] = dot(qf, m, 0, 0)
        emit(ATT, g, i, b, normed)

    def back_local(g, i, b):
        c = place(g, i)
        m, qf, kf, v = m_ref[b, :, c], qf_ref[b, :, c], kf_ref[b, :, c], loc[V, b, :, c]
        ph, plo = split(outside(0, g, i, b))
        s = jnp.where(causal, dot(m, v, 1, 1), 0.0).astype(BF)
        st = jnp.where(causal_t, dot(v, m, 1, 1), 0.0).astype(BF)
        yield
        qg = dot(m, ph, 1, 1) + dot(m, plo, 1, 1) + dot(s, kf, 1, 0)
        dkl_ref[b, :, c] = dot(st, qf, 1, 0)
        dvl_ref[b, :, c] = dot(sct_ref[b, :, c], m, 1, 0)
        yield
        qp = (qg * sq_ref[b, :, c]).astype(BF)
        yield
        wl_ref[b, c, :] = dot(loc[Q, b, :, c], qp, 0, 0)
        emit(DQ, g, i, b, dot(qp, weight(g, i), 1, 1))

    def back_final(g, i, b):
        c = place(g, i)
        qh, ql = split(outside(1, g, i, b))
        v = loc[V, b, :, c]
        yield
        kg = dot(v, qh, 1, 1) + dot(v, ql, 1, 1) + dkl_ref[b, :, c]
        yield
        kp = (kg * sk_ref[b, :, c]).astype(BF)
        kp_ref[b, :, c] = kp
        yield
        wl_ref[b, c, :] += dot(loc[K, b, :, c], kp, 0, 0)

    def back_rest(g, i, b):
        c = place(g, i)
        qh, ql = split(outside(1, g, i, b))
        kf = kf_ref[b, :, c]
        yield
        dv = dot(kf, qh, 1, 0) + dot(kf, ql, 1, 0) + dvl_ref[b, :, c]
        dk = dot(kp_ref[b, :, c], weight(g, i), 1, 1)
        yield
        emit(DV, g, i, b, dv)
        emit(DK, g, i, b, dk)

    def part(o):
        return pl.ds(pl.multiple_of(o * piece, piece), piece)

    def scan_gather(e, g):
        c = pl.ds(g * rows, rows)
        pair[e, g] = state[e, 0, c, :] + state[e, 1, c, :]
        for d in FAR_FIRST:
            o, where = plane(*d)
            remote(
                pair.at[e, g, part(o), :], gat.at[e, g, chip],
                s_gat.at[e, g], r_gat.at[e, g], where,
            ).start()
        gat[e, g, chip] = pair[e, g, part(chip), :]

    def scan_return(e, g):
        bulk(gat.at[e, g, pl.ds(0, n_chip - 1)], s_gat.at[e, g], r_gat.at[e, g]).wait_recv()
        order = range(n_chip) if e == 0 else range(n_chip - 1, -1, -1)
        total = jnp.zeros((piece, HEAD), F32)
        for p in order:
            pre[e, g, p] = total
            total = total + gat[e, g, p]
        for d in FAR_FIRST:
            o, where = plane(*d)
            remote(
                pre.at[e, g, o], ret.at[e, g, part(chip), :],
                s_ret.at[e, g], r_ret.at[e, g], where,
            ).start()
        ret[e, g, part(chip), :] = pre[e, g, chip]

    def scan_wait(e, g):
        bulk(
            ret.at[e, g, pl.ds(0, rows - piece), :], s_ret.at[e, g], r_ret.at[e, g]
        ).wait_recv()

    def weight_parts(g):
        for i in range(PER):
            h = head(core, g, i)
            for c in range(2):
                yield i, c, (dp, 2 * h + c), (chip == h) & (core == c)

    def weight_send(g):
        for i in range(PER):
            wl_ref[0, place(g, i), :] += wl_ref[1, place(g, i), :]
        for i, c, where, own in weight_parts(g):
            part_rows = pl.ds((g * PER + i) * HEAD + c * hw, hw)

            @pl.when(jnp.logical_not(own))
            def _():
                remote(
                    wl_ref.at[0, part_rows, :], wgat.at[chip], s_wg.at[g, i, c], r_wg, where
                ).start()

            @pl.when(own)
            def _():
                wgat[chip] = wl_ref[0, part_rows, :]

    def weight_sum():
        own = core == lax.div(chip, n_chip // 2)

        @pl.when(own)
        def _():
            bulk(wgat.at[pl.ds(0, n_chip - 1)], s_z, r_wg).wait_recv()

        @pl.when(jnp.logical_not(own))
        def _():
            bulk(wgat, s_z, r_wg).wait_recv()

        total = wgat[0]
        for p in range(1, n_chip):
            total = total + wgat[p]
        zsrc[...] = total
        for z in range(n_dp):

            @pl.when(z != dp)
            def _():
                remote(zsrc, zgat.at[dp], s_z, r_z, (z, ctx)).start()

        zgat[dp] = total

    def weight_finish():
        bulk(zgat.at[pl.ds(0, n_dp - 1)], s_z, r_z).wait_recv()
        total = zgat[0]
        for z in range(1, n_dp):
            total = total + zgat[z]
        wg_ref[...] = total

    stores = []

    def store(o, dst):
        c = pltpu.make_async_copy(res.at[o], dst.at[0], out_sem.at[o])
        c.start()
        stores.append(c)

    first = [False] * 3

    def once(i, action):
        if not first[i]:
            first[i] = True
            action()

    def step(name, g):
        if name == "fs":
            once(0, lambda: (loads[K].wait(), loads[V].wait(), w_load.wait()))
            lockstep(g, forward_state, (True, False))
        elif name == "ss":
            once(1, enter)
            swap_state(g).start()
        elif name == "gs":
            swap_state(g).wait_recv()
            scan_gather(0, g)
        elif name == "pk":
            pack(K, g)
            pack(V, g)
            keep(K, g)
            keep(V, g)
        elif name == "pq":
            once(2, lambda: (loads[Q].wait(), loads[G].wait()))
            pack(Q, g)
            pack(G, g)
            keep(Q, g)
            keep(G, g)
        elif name == "kf":
            unpack(K, g)
            unpack(V, g)
            lockstep(g, key_side, (1,))
        elif name == "fl":
            unpack(Q, g)
            unpack(G, g)
            lockstep(g, forward_local)
        elif name == "c0":
            scan_return(0, g)
        elif name == "nu":
            scan_wait(0, g)
            lockstep(g, numer)
            scan_gather(1, g)
            send_back(ATT, g)
        elif name == "bl":
            lockstep(g, back_local)
            send_back(DQ, g)
        elif name == "c1":
            scan_return(1, g)
        elif name == "bf":
            scan_wait(1, g)
            lockstep(g, back_final)
            weight_send(g)
        elif name == "br":
            lockstep(g, back_rest)
            send_back(DK, g)
            send_back(DV, g)

    for word in ORDER:
        if word == "relay":
            relay()
        elif word == "relayed":
            relayed()
        else:
            step(word[:-1], int(word[-1]))
    weight_sum()
    for g in range(GROUPS):
        take_back(ATT, g)
        take_back(DQ, g)
    store(ATT, att_hbm)
    store(DQ, dq_hbm)
    for g in range(GROUPS):
        take_back(DK, g)
        take_back(DV, g)
    store(DK, dk_hbm)
    store(DV, dv_hbm)
    weight_finish()
    wg_out = pltpu.make_async_copy(wg_ref, wg_hbm, w_sem)
    wg_out.start()

    for g in range(GROUPS):
        swap_state(g).wait_send()
        for a in range(4):
            bulk(give.at[a, g], s_in.at[a, g], r_in.at[a, g]).wait_send()
            bulk(back.at[a, g], s_back.at[a, g], r_back.at[a, g]).wait_send()
        for e in range(2):
            bulk(gat.at[e, g, pl.ds(0, n_chip - 1)], s_gat.at[e, g], r_gat.at[e, g]).wait_send()
            bulk(pre.at[e, g, pl.ds(0, n_chip - 1)], s_ret.at[e, g], r_ret.at[e, g]).wait_send()
        for i, c, where, own in weight_parts(g):

            @pl.when(jnp.logical_not(own))
            def _():
                bulk(zsrc, s_wg.at[g, i, c], r_wg).wait_send()

    bulk(zgat.at[pl.ds(0, n_dp - 1)], s_z, r_z).wait_send()
    for c in stores:
        c.wait()
    wg_out.wait()


def body(n_dp, q, k, v, g, w):
    _, tok, width = q.shape
    mine = GROUPS * PER * HEAD
    rows = PER * HEAD
    n_chip = SIDE * SIDE
    hw = HEAD // 2
    dma = pltpu.SemaphoreType.DMA
    act = pltpu.VMEM((2, tok, mine), BF)
    wide = pltpu.VMEM((2, tok, mine), F32)
    moved = pltpu.VMEM((4, GROUPS, PER, tok, HEAD), F32)
    block = pltpu.VMEM((2, GROUPS, rows, HEAD), F32)
    slots = pltpu.VMEM((2, GROUPS, n_chip, rows // n_chip, HEAD), F32)
    part = pltpu.VMEM((hw, HEAD), F32)
    scratch = (
        [pltpu.VMEM((4, tok, width), BF), pltpu.VMEM((width, HEAD), BF)]
        + [pltpu.VMEM((4, tok, width), BF), part]
        + [pltpu.VMEM((4, 2, tok, mine), BF)] + [moved] * 4
        + [act] * 5 + [wide] * 5
        + [pltpu.VMEM((2, 2, mine, HEAD), F32), pltpu.VMEM((GROUPS, rows, HEAD), F32), block, slots, slots, block]
        + [pltpu.VMEM((2, mine, HEAD), F32), pltpu.VMEM((n_chip, hw, HEAD), F32)]
        + [part, pltpu.VMEM((n_dp, hw, HEAD), F32)]
        + [dma((4,)), dma, dma((4,))]
        + [dma((4, GROUPS))] * 4 + [dma((2, GROUPS))] * 4
        + [dma((GROUPS,))] * 2 + [dma((GROUPS, PER, 2)), dma, dma, dma]
        + [pltpu.SemaphoreType.REGULAR] * 2
    )
    outs = [jax.ShapeDtypeStruct(q.shape, BF)] * 4 + [jax.ShapeDtypeStruct((hw, HEAD), F32)]
    hbm = pl.BlockSpec(memory_space=pl.ANY)
    limit = 63 * 1024 * 1024
    results = pl.pallas_call(
        functools.partial(kernel, n_dp, tok),
        out_shape=outs,
        in_specs=[hbm] * 5,
        out_specs=[hbm] * 5,
        scratch_shapes=scratch,
        compiler_params=pltpu.CompilerParams(
            collective_id=0, has_side_effects=True, vmem_limit_bytes=limit
        ),
        cost_estimate=pl.CostEstimate(
            flops=80 * mine * HEAD**2, bytes_accessed=5 * 2**20, transcendentals=0
        ),
    )(q, k, v, g, w)
    return pl.pallas_call(
        write_out,
        out_shape=outs,
        in_specs=[hbm] * 5,
        out_specs=[hbm] * 5,
        scratch_shapes=[pltpu.VMEM(o.shape, o.dtype) for o in outs] + [dma((2, 5))],
        compiler_params=pltpu.CompilerParams(vmem_limit_bytes=limit),
    )(*results)


def solution(mesh):
    spec = P("dp", "ctx", None)
    return jax.shard_map(
        functools.partial(body, mesh.shape["dp"]),
        mesh=mesh,
        in_specs=(spec, spec, spec, spec, P()),
        out_specs=(spec, spec, spec, spec, P("ctx", None)),
        check_vma=False,
    )
```

```python
import functools

import jax
import jax.numpy as jnp
from jax import lax
from jax.experimental import pallas as pl
from jax.experimental.pallas import tpu as pltpu
from jax.sharding import PartitionSpec as P

HEAD = 128
ORDER = (
    "fs0", "fs1", "fs2", "fs3", "ss0", "ss1", "ss2", "ss3", "gs0", "gs1", "gs2", "gs3", "pk0",
    "pk1", "pq0", "pq1", "pk2", "pk3", "pq2", "pq3", "kf0", "fl0", "kf1", "c00", "fl1", "c01",
    "kf2", "c02", "fl2", "c03", "kf3", "fl3", "relay", "nu0", "nu1", "nu2", "nu3", "relayed",
    "bl0", "c10", "bl1", "c11", "bl2", "c12", "bl3", "c13", "bf0", "bf1", "bf2", "bf3", "br0",
    "br1", "br2", "br3",
)
EPS = 1e-05
SIDE = 4
GROUPS = 4
PER = 2
FAR_FIRST = sorted(
    [(x, y) for x in range(SIDE) for y in range(SIDE) if x or y],
    key=lambda d: -sum(min(s, SIDE - s) for s in d),
)
MESH = pl.DeviceIdType.MESH
BF = jnp.bfloat16
F32 = jnp.float32
K, V, Q, G = range(4)
ATT, DQ, DK, DV = range(4)


def dot(a, b, ca, cb):
    return lax.dot_general(a, b, (((ca,), (cb,)), ((), ())), preferred_element_type=F32)


def split(x):
    high = x.astype(BF)
    return high, (x - high.astype(F32)).astype(BF)


def phi(z):
    return jnp.where(z > 0.0, z + 1.0, jnp.exp(jnp.minimum(z, 0.0)))


def write_out(*refs):
    src, dst, mid, sems = refs[:5], refs[5:10], refs[10:15], refs[15]
    ins = [pltpu.make_async_copy(src[i], mid[i], sems.at[0, i]) for i in range(5)]
    outs = [pltpu.make_async_copy(mid[i], dst[i], sems.at[1, i]) for i in range(5)]
    for c in ins:
        c.start()
    for a, b in zip(ins, outs):
        a.wait()
        b.start()
    for c in outs:
        c.wait()


def kernel(
    n_dp, tok,
    q_hbm, k_hbm, v_hbm, g_hbm, w_hbm,
    att_hbm, dq_hbm, dk_hbm, dv_hbm, wg_hbm,
    raw, w_ref, res, wg_ref,
    loc, give, got, back, came,
    qf_ref, kf_ref, sct_ref, m_ref, kp_ref, sq_ref, sk_ref, nl_ref, dkl_ref, dvl_ref,
    state, lent, pair, gat, pre, ret,
    wl_ref, wgat, zsrc, zgat,
    in_sem, w_sem, out_sem,
    s_in, r_in, s_back, r_back, s_gat, r_gat, s_ret, r_ret,
    s_lent, r_lent, s_wg, r_wg, s_z, r_z, near_sem, far_sem,
):
    dp = lax.axis_index("dp")
    ctx = lax.axis_index("ctx")
    core = lax.rem(ctx, 2)
    chip = lax.div(ctx, 2)
    cx, cy = lax.div(chip, SIDE), lax.rem(chip, SIDE)
    near = (dp, ctx + 1 - 2 * core)
    n_chip = SIDE * SIDE
    rows = PER * HEAD
    piece = rows // n_chip
    hw = HEAD // 2

    def plane(dx, dy):
        o = lax.rem(cx + dx, SIDE) * SIDE + lax.rem(cy + dy, SIDE)
        return o, (dp, o * 2 + core)

    def zline(d):
        return (lax.rem(dp + d, n_dp), ctx)

    def remote(src, dst, ssem, rsem, where):
        return pltpu.make_async_remote_copy(
            src_ref=src, dst_ref=dst, send_sem=ssem, recv_sem=rsem,
            device_id=where, device_id_type=MESH,
        )

    def bulk(buf, ssem, rsem):
        return remote(buf, buf, ssem, rsem, near)

    def head(c, g, i):
        n = 2 * c + i
        return SIDE * n + lax.rem(n + g, SIDE)

    def cols(h):
        return pl.ds(pl.multiple_of(h * HEAD, HEAD), HEAD)

    def place(g, i):
        return pl.ds((g * PER + i) * HEAD, HEAD)

    w_load = pltpu.make_async_copy(w_hbm, w_ref, w_sem)
    loads = [
        pltpu.make_async_copy(src.at[0], raw.at[a], in_sem.at[a])
        for a, src in ((K, k_hbm), (V, v_hbm), (Q, q_hbm), (G, g_hbm))
    ]
    loads[K].start()
    loads[V].start()
    w_load.start()

    barrier = pltpu.get_barrier_semaphore()

    def greet(sem, where):
        pl.semaphore_signal(sem, inc=1, device_id=where, device_id_type=MESH)

    for d in FAR_FIRST:
        greet(barrier, plane(*d)[1])
    greet(barrier, near)
    greet(barrier, zline(1))
    greet(barrier, zline(n_dp - 1))

    def enter():
        loads[Q].start()
        loads[G].start()
        pl.semaphore_wait(barrier, 1 + len(FAR_FIRST) + 2)
        greet(near_sem, zline(1))
        greet(near_sem, zline(n_dp - 1))

    def relay():
        pl.semaphore_wait(near_sem, 2)
        greet(far_sem, zline(2))
        greet(far_sem, zline(n_dp - 2))

    def relayed():
        pl.semaphore_wait(far_sem, 2)

    rowid = lax.broadcasted_iota(jnp.int32, (tok, tok), 0)
    colid = lax.broadcasted_iota(jnp.int32, (tok, tok), 1)
    causal = rowid >= colid
    causal_t = rowid <= colid

    def lockstep(g, body, blocks=(0, 1)):
        running = [body(g, i, b) for i in range(PER) for b in blocks]
        while running:
            alive = []
            for r in running:
                try:
                    next(r)
                    alive.append(r)
                except StopIteration:
                    pass
            running = alive

    def pack(a, g):
        for i in range(PER):
            give[a, g, i] = raw[a, :, cols(head(1 - core, g, i))].astype(F32)
        remote(give.at[a, g], got.at[a, g], s_in.at[a, g], r_in.at[a, g], near).start()

    def keep(a, g):
        for i in range(PER):
            loc[a, 0, :, place(g, i)] = raw[a, :, cols(head(core, g, i))]

    def unpack(a, g):
        bulk(got.at[a, g], s_in.at[a, g], r_in.at[a, g]).wait_recv()
        for i in range(PER):
            loc[a, 1, :, place(g, i)] = got[a, g, i].astype(BF)

    def emit(o, g, i, b, value):
        if b == 0:
            res[o, :, cols(head(core, g, i))] = value.astype(BF)
        else:
            back[o, g, i] = value

    def send_back(o, g):
        remote(back.at[o, g], came.at[o, g], s_back.at[o, g], r_back.at[o, g], near).start()

    def take_back(o, g):
        bulk(came.at[o, g], s_back.at[o, g], r_back.at[o, g]).wait_recv()
        for i in range(PER):
            res[o, :, cols(head(1 - core, g, i))] = came[o, g, i].astype(BF)

    def weight(g, i):
        return w_ref[cols(head(core, g, i)), :]

    def outside(e, g, i, b):
        use = (core == 1) if e == b else (core == 0)
        other = state[e, 1 - b, place(g, i), :]
        return ret[e, g, pl.ds(i * HEAD, HEAD), :] + jnp.where(use, other, 0.0)

    def key_side(g, i, b):
        c = place(g, i)
        z = dot(loc[K, b, :, c], weight(g, i), 1, 0)
        yield
        f = phi(z)
        kf_ref[b, :, c] = f.astype(BF)
        sk_ref[b, :, c] = jnp.minimum(f, 1.0)

    def forward_state(g, i, own):
        c = cols(head(core if own else 1 - core, g, i))
        z = dot(raw[K, :, c], w_ref[c, :], 1, 0)
        yield
        f = phi(z)
        kf = f.astype(BF)
        if own:
            kf_ref[0, :, place(g, i)] = kf
            sk_ref[0, :, place(g, i)] = jnp.minimum(f, 1.0)
        yield
        s = dot(kf, raw[V, :, c], 0, 0)
        if own:
            state[0, 0, place(g, i), :] = s
        else:
            lent[g, pl.ds(i * HEAD, HEAD), :] = s

    def swap_state(g):
        return remote(
            lent.at[g], state.at[0, 1, pl.ds(g * rows, rows), :], s_lent.at[g], r_lent.at[g], near
        )

    def forward_local(g, i, b):
        c = place(g, i)
        z = dot(loc[Q, b, :, c], weight(g, i), 1, 0)
        yield
        f = phi(z)
        qf = f.astype(BF)
        qf_ref[b, :, c] = qf
        sq_ref[b, :, c] = jnp.minimum(f, 1.0)
        yield
        kf = kf_ref[b, :, c]
        w = jnp.where(causal, dot(qf, kf, 1, 1), 0.0).astype(BF)
        sct_ref[b, :, c] = jnp.where(causal_t, dot(kf, qf, 1, 1), 0.0).astype(BF)
        yield
        nl_ref[b, :, c] = dot(w, loc[V, b, :, c], 1, 0)

    def numer(g, i, b):
        c = place(g, i)
        qf = qf_ref[b, :, c]
        ph, plo = split(outside(0, g, i, b))
        yield
        n = dot(qf, ph, 1, 0) + dot(qf, plo, 1, 0) + nl_ref[b, :, c]
        yield
        r = lax.rsqrt(jnp.mean(n * n, axis=-1, keepdims=True) + EPS)
        yield
        normed = n * r
        nl_ref[b, :, c] = normed
        og = loc[G, b, :, c].astype(F32)
        s = jnp.mean(og * normed, axis=-1, keepdims=True)
        yield
        m = (r * (og - normed * s)).astype(BF)
        m_ref[b, :, c] = m
        yield
        state[1, b, c, :] = dot(qf, m, 0, 0)

    def attend(g, i, b):
        emit(ATT, g, i, b, nl_ref[b, :, place(g, i)])
        yield

    def back_local(g, i, b):
        c = place(g, i)
        m, qf, kf, v = m_ref[b, :, c], qf_ref[b, :, c], kf_ref[b, :, c], loc[V, b, :, c]
        ph, plo = split(outside(0, g, i, b))
        s = jnp.where(causal, dot(m, v, 1, 1), 0.0).astype(BF)
        st = jnp.where(causal_t, dot(v, m, 1, 1), 0.0).astype(BF)
        yield
        qg = dot(m, ph, 1, 1) + dot(m, plo, 1, 1) + dot(s, kf, 1, 0)
        dkl_ref[b, :, c] = dot(st, qf, 1, 0)
        dvl_ref[b, :, c] = dot(sct_ref[b, :, c], m, 1, 0)
        yield
        qp = (qg * sq_ref[b, :, c]).astype(BF)
        yield
        wl_ref[b, c, :] = dot(loc[Q, b, :, c], qp, 0, 0)
        emit(DQ, g, i, b, dot(qp, weight(g, i), 1, 1))

    def back_final(g, i, b):
        c = place(g, i)
        qh, ql = split(outside(1, g, i, b))
        v = loc[V, b, :, c]
        yield
        kg = dot(v, qh, 1, 1) + dot(v, ql, 1, 1) + dkl_ref[b, :, c]
        yield
        kp = (kg * sk_ref[b, :, c]).astype(BF)
        kp_ref[b, :, c] = kp
        yield
        wl_ref[b, c, :] += dot(loc[K, b, :, c], kp, 0, 0)

    def back_rest(g, i, b):
        c = place(g, i)
        qh, ql = split(outside(1, g, i, b))
        kf = kf_ref[b, :, c]
        yield
        dv = dot(kf, qh, 1, 0) + dot(kf, ql, 1, 0) + dvl_ref[b, :, c]
        dk = dot(kp_ref[b, :, c], weight(g, i), 1, 1)
        yield
        emit(DV, g, i, b, dv)
        emit(DK, g, i, b, dk)

    def part(o):
        return pl.ds(pl.multiple_of(o * piece, piece), piece)

    def scan_gather(e, g):
        c = pl.ds(g * rows, rows)
        pair[e, g] = state[e, 0, c, :] + state[e, 1, c, :]
        for d in FAR_FIRST:
            o, where = plane(*d)
            remote(
                pair.at[e, g, part(o), :], gat.at[e, g, chip],
                s_gat.at[e, g], r_gat.at[e, g], where,
            ).start()
        gat[e, g, chip] = pair[e, g, part(chip), :]

    def scan_return(e, g):
        bulk(gat.at[e, g, pl.ds(0, n_chip - 1)], s_gat.at[e, g], r_gat.at[e, g]).wait_recv()
        order = range(n_chip) if e == 0 else range(n_chip - 1, -1, -1)
        total = jnp.zeros((piece, HEAD), F32)
        for p in order:
            pre[e, g, p] = total
            total = total + gat[e, g, p]
        for d in FAR_FIRST:
            o, where = plane(*d)
            remote(
                pre.at[e, g, o], ret.at[e, g, part(chip), :],
                s_ret.at[e, g], r_ret.at[e, g], where,
            ).start()
        ret[e, g, part(chip), :] = pre[e, g, chip]

    def scan_wait(e, g):
        bulk(
            ret.at[e, g, pl.ds(0, rows - piece), :], s_ret.at[e, g], r_ret.at[e, g]
        ).wait_recv()

    def weight_parts(g):
        for i in range(PER):
            h = head(core, g, i)
            for c in range(2):
                yield i, c, (dp, 2 * h + c), (chip == h) & (core == c)

    def weight_send(g):
        for i in range(PER):
            wl_ref[0, place(g, i), :] += wl_ref[1, place(g, i), :]
        for i, c, where, own in weight_parts(g):
            part_rows = pl.ds((g * PER + i) * HEAD + c * hw, hw)

            @pl.when(jnp.logical_not(own))
            def _():
                remote(
                    wl_ref.at[0, part_rows, :], wgat.at[chip], s_wg.at[g, i, c], r_wg, where
                ).start()

            @pl.when(own)
            def _():
                wgat[chip] = wl_ref[0, part_rows, :]

    def weight_sum():
        own = core == lax.div(chip, n_chip // 2)

        @pl.when(own)
        def _():
            bulk(wgat.at[pl.ds(0, n_chip - 1)], s_z, r_wg).wait_recv()

        @pl.when(jnp.logical_not(own))
        def _():
            bulk(wgat, s_z, r_wg).wait_recv()

        total = wgat[0]
        for p in range(1, n_chip):
            total = total + wgat[p]
        zsrc[...] = total
        for z in range(n_dp):

            @pl.when(z != dp)
            def _():
                remote(zsrc, zgat.at[dp], s_z, r_z, (z, ctx)).start()

        zgat[dp] = total

    def weight_finish():
        bulk(zgat.at[pl.ds(0, n_dp - 1)], s_z, r_z).wait_recv()
        total = zgat[0]
        for z in range(1, n_dp):
            total = total + zgat[z]
        wg_ref[...] = total

    stores = []

    def store(o, dst):
        c = pltpu.make_async_copy(res.at[o], dst.at[0], out_sem.at[o])
        c.start()
        stores.append(c)

    first = [False] * 3

    def once(i, action):
        if not first[i]:
            first[i] = True
            action()

    def step(name, g):
        if name == "fs":
            once(0, lambda: (loads[K].wait(), loads[V].wait(), w_load.wait()))
            lockstep(g, forward_state, (True, False))
        elif name == "ss":
            once(1, enter)
            swap_state(g).start()
        elif name == "gs":
            swap_state(g).wait_recv()
            scan_gather(0, g)
        elif name == "pk":
            pack(K, g)
            pack(V, g)
            keep(K, g)
            keep(V, g)
        elif name == "pq":
            once(2, lambda: (loads[Q].wait(), loads[G].wait()))
            pack(Q, g)
            pack(G, g)
            keep(Q, g)
            keep(G, g)
        elif name == "kf":
            unpack(K, g)
            unpack(V, g)
            lockstep(g, key_side, (1,))
        elif name == "fl":
            unpack(Q, g)
            unpack(G, g)
            lockstep(g, forward_local)
        elif name == "c0":
            scan_return(0, g)
        elif name == "nu":
            scan_wait(0, g)
            lockstep(g, numer)
            scan_gather(1, g)
            lockstep(g, attend)
            send_back(ATT, g)
        elif name == "bl":
            lockstep(g, back_local)
            send_back(DQ, g)
        elif name == "c1":
            scan_return(1, g)
        elif name == "bf":
            scan_wait(1, g)
            lockstep(g, back_final)
            weight_send(g)
        elif name == "br":
            lockstep(g, back_rest)
            send_back(DK, g)
            send_back(DV, g)

    for word in ORDER:
        if word == "relay":
            relay()
        elif word == "relayed":
            relayed()
        else:
            step(word[:-1], int(word[-1]))
    weight_sum()
    for g in range(GROUPS):
        take_back(ATT, g)
        take_back(DQ, g)
    store(ATT, att_hbm)
    store(DQ, dq_hbm)
    for g in range(GROUPS):
        take_back(DK, g)
        take_back(DV, g)
    store(DK, dk_hbm)
    store(DV, dv_hbm)
    weight_finish()
    wg_out = pltpu.make_async_copy(wg_ref, wg_hbm, w_sem)
    wg_out.start()

    for g in range(GROUPS):
        swap_state(g).wait_send()
        for a in range(4):
            bulk(give.at[a, g], s_in.at[a, g], r_in.at[a, g]).wait_send()
            bulk(back.at[a, g], s_back.at[a, g], r_back.at[a, g]).wait_send()
        for e in range(2):
            bulk(gat.at[e, g, pl.ds(0, n_chip - 1)], s_gat.at[e, g], r_gat.at[e, g]).wait_send()
            bulk(pre.at[e, g, pl.ds(0, n_chip - 1)], s_ret.at[e, g], r_ret.at[e, g]).wait_send()
        for i, c, where, own in weight_parts(g):

            @pl.when(jnp.logical_not(own))
            def _():
                bulk(zsrc, s_wg.at[g, i, c], r_wg).wait_send()

    bulk(zgat.at[pl.ds(0, n_dp - 1)], s_z, r_z).wait_send()
    for c in stores:
        c.wait()
    wg_out.wait()


def body(n_dp, q, k, v, g, w):
    _, tok, width = q.shape
    mine = GROUPS * PER * HEAD
    rows = PER * HEAD
    n_chip = SIDE * SIDE
    hw = HEAD // 2
    dma = pltpu.SemaphoreType.DMA
    act = pltpu.VMEM((2, tok, mine), BF)
    wide = pltpu.VMEM((2, tok, mine), F32)
    moved = pltpu.VMEM((4, GROUPS, PER, tok, HEAD), F32)
    block = pltpu.VMEM((2, GROUPS, rows, HEAD), F32)
    slots = pltpu.VMEM((2, GROUPS, n_chip, rows // n_chip, HEAD), F32)
    part = pltpu.VMEM((hw, HEAD), F32)
    scratch = (
        [pltpu.VMEM((4, tok, width), BF), pltpu.VMEM((width, HEAD), BF)]
        + [pltpu.VMEM((4, tok, width), BF), part]
        + [pltpu.VMEM((4, 2, tok, mine), BF)] + [moved] * 4
        + [act] * 5 + [wide] * 5
        + [pltpu.VMEM((2, 2, mine, HEAD), F32), pltpu.VMEM((GROUPS, rows, HEAD), F32), block, slots, slots, block]
        + [pltpu.VMEM((2, mine, HEAD), F32), pltpu.VMEM((n_chip, hw, HEAD), F32)]
        + [part, pltpu.VMEM((n_dp, hw, HEAD), F32)]
        + [dma((4,)), dma, dma((4,))]
        + [dma((4, GROUPS))] * 4 + [dma((2, GROUPS))] * 4
        + [dma((GROUPS,))] * 2 + [dma((GROUPS, PER, 2)), dma, dma, dma]
        + [pltpu.SemaphoreType.REGULAR] * 2
    )
    outs = [jax.ShapeDtypeStruct(q.shape, BF)] * 4 + [jax.ShapeDtypeStruct((hw, HEAD), F32)]
    hbm = pl.BlockSpec(memory_space=pl.ANY)
    limit = 63 * 1024 * 1024
    results = pl.pallas_call(
        functools.partial(kernel, n_dp, tok),
        out_shape=outs,
        in_specs=[hbm] * 5,
        out_specs=[hbm] * 5,
        scratch_shapes=scratch,
        compiler_params=pltpu.CompilerParams(
            collective_id=0, has_side_effects=True, vmem_limit_bytes=limit
        ),
        cost_estimate=pl.CostEstimate(
            flops=80 * mine * HEAD**2, bytes_accessed=5 * 2**20, transcendentals=0
        ),
    )(q, k, v, g, w)
    return pl.pallas_call(
        write_out,
        out_shape=outs,
        in_specs=[hbm] * 5,
        out_specs=[hbm] * 5,
        scratch_shapes=[pltpu.VMEM(o.shape, o.dtype) for o in outs] + [dma((2, 5))],
        compiler_params=pltpu.CompilerParams(vmem_limit_bytes=limit),
    )(*results)


def solution(mesh):
    spec = P("dp", "ctx", None)
    return jax.shard_map(
        functools.partial(body, mesh.shape["dp"]),
        mesh=mesh,
        in_specs=(spec, spec, spec, spec, P()),
        out_specs=(spec, spec, spec, spec, P("ctx", None)),
        check_vma=False,
    )
```
